512 devices in a mesh: mode: 128 (over y, z, core), mer: 4 (over x).
Axes of the slice: x: 4, y: 8, z: 8, core: 2. Of those that a mesh axis runs over, the one named last changes fastest.
Arguments:
- mode_cost: int32 [512], replicated, may hold values from 105 to 420, as said below
- iface_index: int32 [128], replicated, may hold values from 0 to 255, as said below
- basis: float32 [4, 2, 1024, 128, 256], P(None, None, 'mode', 'mer'), as said below
- radial: float32 [2, 256, 256], replicated, as said below
- axial: float32 [2, 128, 32], P(None, 'mer'), as said below
- flow_coupling: float32 [4, 128, 256], P(None, 'mer'), may hold values from -8 to 8
- swirl: float32 [128, 256], P('mer'), may hold values from -6 to 6
- shift: float32 [2], replicated, may hold values from 0.2 to 0.8
Outputs:
- new_vector: float32 [2, 1024, 128, 256], P(None, 'mode', 'mer')
- coeffs: float32 [2, 4], replicated
- norm: float32 [], replicated
The draws below stay inside these ranges and needn't reach their ends.
Inputs may be any that keep to these rules, and one draw needn't show every extreme that they name: `mode_cost`: every group has 2 to 8 modes and one group has exactly 8; within a group all costs are equal. `iface_index`: distinct and increasing; the first is 0 and the last is 255. `basis`: entries of order one to some tens. `radial`: each matrix has a unit diagonal plus entries of order 1 / sqrt(256). `axial`: each block has a unit diagonal plus entries of order 1 / sqrt(32).
All inputs are finite; a program needn't handle non-finite values.
Results may differ from the reference program's by a relative error of at most 0.000075.
Values sent between devices are 32-bit elements; how exact they have to be, the bound alone decides.
No kernel may reach another device: no remote copies, remote signals or barrier semaphores. Data moves between devices by JAX's collectives and lax.ppermute only.
A program may use at most 64 MiB of HBM per device.

```python
import jax
import jax.numpy as jnp
from jax import lax

NR = 256
IFACE = 128
NZ_DEV = 32
MODES_DEV = 4
SLOTS = 8
KRYLOV = 4
QUOTA = 840
MODES = 512
NZ = 128
N_MODE = 128
N_MER = 4


def draw_mode_cost(key, part):
    groups = MODES // MODES_DEV
    pairs = groups // 2
    key_delta = jax.random.fold_in(key, 11)
    key_pick = jax.random.fold_in(key, 12)
    delta = jax.random.randint(key_delta, (pairs,), -2, 3)
    picked = jax.random.randint(key_pick, (), 0, pairs)
    partner = (picked + 1) % pairs
    places = jnp.arange(pairs)
    first = MODES_DEV + delta
    second = MODES_DEV - delta
    first = jnp.where(places == picked, SLOTS, jnp.where(places == partner, 2, first))
    second = jnp.where(places == picked, 2, jnp.where(places == partner, 2 * MODES_DEV - 2, second))
    sizes = jnp.stack([first, second], axis=1).reshape(groups).astype(jnp.int32)
    ends = jnp.cumsum(sizes)
    modes = jnp.arange(MODES)
    group = jnp.sum((modes[:, None] >= ends[None, :]).astype(jnp.int32), axis=1)
    return (QUOTA // sizes[group]).astype(jnp.int32)


def draw_iface_index(key, part):
    inner = jax.random.permutation(jax.random.fold_in(key, 21), NR - 2)[:IFACE - 2] + 1
    ends = jnp.array([0, NR - 1], dtype=jnp.int32)
    return jnp.sort(jnp.concatenate([ends, inner.astype(jnp.int32)]))


def draw_basis(key, part):
    total_slots = MODES // MODES_DEV * SLOTS
    shape = (KRYLOV, 2, total_slots, NZ, NR)
    key_common = jax.random.fold_in(key, 31)
    key_own = jax.random.fold_in(key, 32)
    key_slot = jax.random.fold_in(key, 33)
    key_rad = jax.random.fold_in(key, 34)
    slot_frac = jax.random.uniform(key_slot, (total_slots,), jnp.float32)
    radial_frac = jax.random.uniform(key_rad, (NR,), jnp.float32)
    common = jax.random.truncated_normal(key_common, -4.0, 4.0, shape[1:], jnp.float32)
    own = jax.random.truncated_normal(key_own, -4.0, 4.0, shape, jnp.float32)
    mixed = 0.6 * common[None] + 0.8 * own
    scale = jnp.exp(jnp.log(10.0) * slot_frac)[:, None, None] * jnp.exp(jnp.log(3.0) * radial_frac)[None, None, :]
    return mixed * scale[None, None]


def draw_radial(key, part):
    key = jax.random.fold_in(key, 41)
    rows = jnp.arange(NR)
    identity = (rows[:, None] == rows[None, :]).astype(jnp.float32)
    noise = jax.random.truncated_normal(key, -4.0, 4.0, (2, NR, NR), jnp.float32)
    return identity[None] + 0.5 * noise / jnp.sqrt(float(NR))


def draw_axial(key, part):
    key = jax.random.fold_in(key, 51)
    rows = jnp.arange(NZ) % NZ_DEV
    cols = jnp.arange(NZ_DEV)
    identity = (rows[:, None] == cols[None, :]).astype(jnp.float32)
    noise = jax.random.truncated_normal(key, -4.0, 4.0, (2, NZ, NZ_DEV), jnp.float32)
    return identity[None] + 0.5 * noise / jnp.sqrt(float(NZ_DEV))


def level_of(stream_key, dims, shards, least, high):
    def one(axis_at, shards_of):
        draws = jax.random.uniform(jax.random.fold_in(jax.random.fold_in(stream_key, 6), axis_at), (shards_of,), jnp.float32, least / len(shards), high / len(shards))
        return jnp.repeat(jnp.exp(draws), dims[axis_at] // shards_of).reshape((-1,) + (1,) * (len(dims) - axis_at - 1))

    factor_of = one(*shards[0])
    for cut in shards[1:]:
        factor_of = factor_of * one(*cut)
    return factor_of


def normal_values(key, shape, width, limit, split=(), kind=jnp.bfloat16):
    entries = width * jax.random.normal(key, shape, jnp.float32)
    if split:
        entries = entries * level_of(key, shape, split, -0.22, 0.18)
    return jnp.clip(entries, -limit, limit).astype(kind)


def setup_inputs(seed: int = 0) -> dict:
    key_list = jax.random.split(jax.random.key(seed), 9)
    mode_cost = draw_mode_cost(jax.random.fold_in(key_list[8], 71), 0)
    iface_index = draw_iface_index(jax.random.fold_in(key_list[8], 71), 0)
    basis = draw_basis(jax.random.fold_in(key_list[8], 71), 0)
    radial = draw_radial(jax.random.fold_in(key_list[8], 71), 0)
    axial = draw_axial(jax.random.fold_in(key_list[8], 71), 0)
    flow_coupling = normal_values(key_list[5], (4, NZ, NR), 2.0, 8.0, ((1, 4),), jnp.float32)
    swirl = normal_values(key_list[6], (NZ, NR), 1.0, 6.0, ((0, 4),), jnp.float32)
    shift = jnp.clip(jax.random.uniform(key_list[7], (2,), jnp.float32, 0.2, 0.8), 0.2, 0.8)
    return {"mode_cost": mode_cost, "iface_index": iface_index, "basis": basis, "radial": radial, "axial": axial, "flow_coupling": flow_coupling, "swirl": swirl, "shift": shift}


penalty = 1.0
schur_diag = 2.2
epsilon = 1e-06

def slot_layout(mode_cost):
    prefix = jnp.cumsum(mode_cost) - mode_cost
    owner = (prefix // QUOTA).astype(jnp.int32)
    devices = jnp.arange(N_MODE, dtype=jnp.int32)
    starts = lax.optimization_barrier(jnp.sum((owner[None, :] < devices[:, None]).astype(jnp.int32), axis=1))
    within = jnp.arange(MODES, dtype=jnp.int32) - starts[owner]
    return (owner * SLOTS + within).astype(jnp.int32)

def solve_interface(rhs):
    count = rhs.shape[0]
    places = jnp.arange(count)
    diagonal = jnp.full((count,), schur_diag, rhs.dtype)
    below = jnp.where(places > 0, -1.0, 0.0).astype(rhs.dtype)
    above = jnp.where(places < count - 1, -1.0, 0.0).astype(rhs.dtype)
    return lax.linalg.tridiagonal_solve(below, diagonal, above, rhs)

def reference(mode_cost, iface_index, basis, radial, axial, flow_coupling, swirl, shift):
    highest = lax.Precision.HIGHEST
    slot_of = slot_layout(mode_cost)
    vectors = jnp.take(basis, slot_of, axis=2)
    current = vectors[KRYLOV - 1]
    radial_term = jnp.einsum('cmzr,tr->cmzt', current, radial[0], precision=highest)
    blocked = current.reshape(2, MODES, N_MER, NZ_DEV, NR)
    block_op = axial[0].reshape(N_MER, NZ_DEV, NZ_DEV)
    block_inv = axial[1].reshape(N_MER, NZ_DEV, NZ_DEV)
    axial_term = jnp.einsum('bij,cmbjr->cmbir', block_op, blocked, precision=highest)
    link = jnp.zeros_like(blocked)
    link = link.at[:, :, 1:, 0].add(blocked[:, :, :-1, -1])
    link = link.at[:, :, :-1, -1].add(blocked[:, :, 1:, 0])
    image = radial_term + (axial_term + penalty * link).reshape(2, MODES, NZ, NR)
    padded = jnp.pad(current, ((0, 0), (2, 2), (0, 0), (0, 0)))
    for which, offset in enumerate((-2, -1, 1, 2)):
        image = image + flow_coupling[which] * padded[:, 2 + offset:2 + offset + MODES]
    wave = jnp.arange(MODES).astype(jnp.float32) / MODES
    rotation = wave[:, None, None] * swirl[None]
    image_re = image[0] - rotation * current[1]
    image_im = image[1] + rotation * current[0]
    shifted_re = image_re - (shift[0] * current[0] - shift[1] * current[1])
    shifted_im = image_im - (shift[0] * current[1] + shift[1] * current[0])
    shifted = jnp.stack([shifted_re, shifted_im]).reshape(2, MODES, N_MER, NZ_DEV, NR)
    local = jnp.einsum('bij,cmbjr->cmbir', block_inv, shifted, precision=highest)
    local = jnp.einsum('cmbir,tr->cmbit', local, radial[1], precision=highest)
    jumps = local[:, :, :-1, -1, :] - local[:, :, 1:, 0, :]
    chosen = jnp.take(jumps, iface_index, axis=3)
    rhs = jnp.moveaxis(chosen, 2, 0)
    solved = solve_interface(rhs.reshape(N_MER - 1, -1)).reshape(rhs.shape)
    zero_row = jnp.zeros((1,) + rhs.shape[1:], rhs.dtype)
    padded_g = jnp.moveaxis(jnp.concatenate([zero_row, solved, zero_row], axis=0), 0, 2)
    position = jnp.arange(NZ_DEV).astype(jnp.float32) / (NZ_DEV - 1)
    lower_w = (1.0 - position)[None, None, None, :, None]
    upper_w = position[None, None, None, :, None]
    correction = lower_w * padded_g[:, :, :-1, None, :] - upper_w * padded_g[:, :, 1:, None, :]
    local = local.at[..., iface_index].add(correction)
    result = local.reshape(2, MODES, NZ, NR)
    dof = float(MODES * NZ * NR)
    proj_re = lax.optimization_barrier(jnp.sum(vectors * result[None], axis=(1, 2, 3, 4))) / dof
    proj_im = lax.optimization_barrier(jnp.sum(vectors[:, 0] * result[None, 1] - vectors[:, 1] * result[None, 0], axis=(1, 2, 3))) / dof
    rest_re = result[0] - lax.optimization_barrier(jnp.sum(proj_re[:, None, None, None] * vectors[:, 0] - proj_im[:, None, None, None] * vectors[:, 1], axis=0))
    rest_im = result[1] - lax.optimization_barrier(jnp.sum(proj_re[:, None, None, None] * vectors[:, 1] + proj_im[:, None, None, None] * vectors[:, 0], axis=0))
    total = (jnp.sum(rest_re * rest_re) + jnp.sum(rest_im * rest_im)) / dof
    norm = jnp.sqrt(total + epsilon)
    fresh = jnp.stack([rest_re, rest_im]) / norm
    new_vector = jnp.zeros((2, N_MODE * SLOTS, NZ, NR), fresh.dtype).at[:, slot_of].set(fresh)
    return (new_vector, jnp.stack([proj_re, proj_im]), norm)
```

```python
import functools
import math

import jax
import jax.numpy as jnp
import numpy as np
from jax import lax
from jax.experimental import pallas as pl
from jax.experimental.pallas import tpu as pltpu
from jax.sharding import Mesh
from jax.sharding import PartitionSpec as P

QUOTA = 840
PENALTY = 1.0
SCHUR_DIAG = 2.2
EPSILON = 1e-06

VMEM = pl.BlockSpec(memory_space=pltpu.VMEM)
ANY = pl.BlockSpec(memory_space=pl.ANY)
SMEM = pl.BlockSpec(memory_space=pltpu.SMEM)
F32 = jnp.float32
BF16 = jnp.bfloat16
NT = (((1,), (1,)), ((), ()))
NN = (((1,), (0,)), ((), ()))


def split(x):
    high = x.astype(BF16)
    return high, (x - high.astype(F32)).astype(BF16)


def dot3(a, b, dims):
    def one(x, y):
        return lax.dot_general(x, y, dims, preferred_element_type=F32)

    return one(a[0], b[0]) + (one(a[0], b[1]) + one(a[1], b[0]))


def block_diagonal(block, copies):
    n = block.shape[0]
    size = n * copies
    rows = lax.broadcasted_iota(jnp.int32, (n, size), 0)
    cols = lax.broadcasted_iota(jnp.int32, (n, size), 1)
    spread = jnp.where(cols % n == rows, 1.0, 0.0).astype(BF16)
    on = (
        lax.broadcasted_iota(jnp.int32, (size, size), 0) // n
        == lax.broadcasted_iota(jnp.int32, (size, size), 1) // n
    )
    parts = []
    for part in split(block):
        tiled = lax.dot_general(part, spread, NN, preferred_element_type=F32)
        tiled = jnp.concatenate([tiled] * copies, axis=0)
        parts.append(jnp.where(on, tiled, 0.0).astype(BF16))
    return parts


def layout_kernel(group_of, krylov, cost_ref, basis_ref, info_ref, other_ref, pair_ref, sems):
    group = group_of()
    even = lax.rem(group, 2) == 0

    def copy(at, ref, which, part):
        return pltpu.make_async_copy(
            basis_ref.at[krylov - 1, part, pl.ds(at, 2)], ref.at[part], sems.at[which, part]
        )

    @pl.when(even)
    def _():
        for part in range(2):
            copy(0, other_ref, 0, part).start()

    @pl.when(jnp.logical_not(even))
    def _():
        for part in range(2):
            copy(0, pair_ref, 0, part).start()

    cost = cost_ref[...]
    rows, lanes = cost.shape
    lane = lax.broadcasted_iota(jnp.int32, cost.shape, 1)
    row = lax.broadcasted_iota(jnp.int32, cost.shape, 0)
    total = cost
    step = 1
    while step < lanes:
        total = total + jnp.where(lane >= step, pltpu.roll(total, step, 1), 0)
        step *= 2
    prefix = total - cost
    for i in range(rows - 1):
        prefix = prefix + jnp.where(row > i, total[i : i + 1, lanes - 1 :], 0)
    base = 2 * rows * lanes
    both = jnp.where(prefix < group * QUOTA, 1.0, 0.0)
    both = both + jnp.where(prefix < (group + 1) * QUOTA, float(base), 0.0)
    both = jnp.sum(both).astype(jnp.int32)
    start = lax.rem(both, base)
    count = lax.div(both, base) - start

    top = jnp.maximum(count - 2, 0)

    @pl.when(even)
    def _():
        for part in range(2):
            copy(top, pair_ref, 1, part).start()

    @pl.when(jnp.logical_not(even))
    def _():
        for part in range(2):
            copy(top, other_ref, 1, part).start()

    info_ref[0] = count
    info_ref[1] = start
    for which in range(2):
        for part in range(2):
            copy(0, pair_ref, which, part).wait()


def inner_kernel(
    modes,
    info_ref,
    iface_ref,
    shift_ref,
    basis_ref,
    radial_ref,
    axial_ref,
    flow_ref,
    swirl_ref,
    local_ref,
    ends_ref,
    block_ref,
    radial1_ref,
    gram_ref,
    mask_ref,
    high_ref,
    low_ref,
):
    krylov, _, slots, points, width = basis_ref.shape
    count = info_ref[0]
    start = info_ref[1]
    rows = slots * points
    last = krylov - 1

    pairs = [(i, j) for i in range(krylov) for j in range(i, krylov)]
    n_sums = sum(1 if i == j else 2 for i, j in pairs)

    def gram_step(slot, sums):
        sums = list(sums)
        for r in range(0, points, 8):
            for c in range(0, width, 128):
                q = [
                    [basis_ref[k, p, slot, r : r + 8, c : c + 128] for p in range(2)]
                    for k in range(krylov)
                ]
                at = 0
                for i, j in pairs:
                    sums[at] = sums[at] + (q[i][0] * q[j][0] + q[i][1] * q[j][1])
                    at += 1
                    if i != j:
                        sums[at] = sums[at] + (q[i][0] * q[j][1] - q[i][1] * q[j][0])
                        at += 1
        return tuple(sums)

    sums = lax.fori_loop(0, count, gram_step, tuple(jnp.zeros((8, 128), F32) for _ in range(n_sums)))
    lane = lax.broadcasted_iota(jnp.int32, (1, 128), 1)
    gram = jnp.zeros((1, 128), F32)
    for i, s in enumerate(sums):
        gram = gram + jnp.where(lane == 2 * krylov + 1 + i, jnp.sum(s, keepdims=True), 0.0)
    gram_ref[...] = gram

    column = lax.broadcasted_iota(jnp.int32, (1, width), 1)

    def mark(i, mask):
        return jnp.where(column == iface_ref[i], 1.0, mask)

    mask_ref[...] = lax.fori_loop(0, iface_ref.shape[0], mark, jnp.zeros((1, width), F32), unroll=8)

    first_block = block_diagonal(axial_ref[0], slots)
    second_block = block_diagonal(axial_ref[1], slots)
    block_ref[0] = second_block[0]
    block_ref[1] = second_block[1]
    radial1 = split(radial_ref[1])
    radial1_ref[0] = radial1[0]
    radial1_ref[1] = radial1[1]
    radial0 = split(radial_ref[0])


    def current(part, slot):
        return jnp.where(slot < count, basis_ref[last, part, slot], 0.0)

    for part in range(2):
        for slot in range(slots):
            high, low = split(current(part, slot))
            high_ref[part, slot * points : (slot + 1) * points] = high
            low_ref[part, slot * points : (slot + 1) * points] = low

    for part in range(2):
        v = (high_ref[part], low_ref[part])
        image = dot3(v, radial0, NT) + dot3(first_block, v, NN)
        local_ref[part] = image.reshape(slots, points, width)

    for which, point in enumerate((points - 1, 0)):
        picked = jnp.concatenate(
            [
                jnp.where(s < count, basis_ref[last, part, s, point : point + 1], 0.0)
                for part in range(2)
                for s in range(slots)
            ],
            axis=0,
        )
        ends_ref[which] = dot3(split(picked), radial1, NT)

    sigma_re = shift_ref[0]
    sigma_im = shift_ref[1]
    for slot in range(slots):
        wave = (start + slot).astype(F32) / modes
        rotation = wave * swirl_ref[...]
        turn = rotation - sigma_im
        v_re = current(0, slot)
        v_im = current(1, slot)
        new = [
            local_ref[0, slot] - turn * v_im - sigma_re * v_re,
            local_ref[1, slot] + turn * v_re - sigma_re * v_im,
        ]
        for which, offset in enumerate((-2, -1, 1, 2)):
            if 0 <= slot + offset < slots:
                for part in range(2):
                    new[part] = new[part] + flow_ref[which] * current(part, slot + offset)
        for part in range(2):
            high, low = split(jnp.where(slot < count, new[part], 0.0))
            high_ref[part, slot * points : (slot + 1) * points] = high
            low_ref[part, slot * points : (slot + 1) * points] = low

    for part in range(2):
        x = (high_ref[part], low_ref[part])
        x = split(dot3(second_block, x, NN))
        local_ref[part] = dot3(x, radial1, NT).reshape(slots, points, width)


def halo_kernel(
    group_of,
    modes,
    info_ref,
    other_ref,
    pair_ref,
    flow_ref,
    block_ref,
    radial1_ref,
    ends_ref,
    axial_ref,
    before_ref,
    local_ref,
    message_ref,
):
    _, slots, points, width = local_ref.shape
    local_ref[...] = before_ref[...]
    count = info_ref[0]
    end = count + info_ref[1]
    group = group_of()
    even = lax.rem(group, 2) == 0
    inputs = []
    for part in range(2):
        lower = [jnp.where(even, other_ref[part, i], pair_ref[part, i]) for i in range(2)]
        upper = [jnp.where(even, pair_ref[part, i], other_ref[part, i]) for i in range(2)]
        lower = [jnp.where(group > 0, x, 0.0) for x in lower]
        upper = [jnp.where(end + i < modes, x, 0.0) for i, x in enumerate(upper)]
        inputs += [
            jnp.where(count > 0, flow_ref[0] * lower[0] + flow_ref[1] * lower[1], 0.0),
            jnp.where(count > 1, flow_ref[0] * lower[1], 0.0),
            flow_ref[3] * upper[0],
            flow_ref[2] * upper[0] + flow_ref[3] * upper[1],
        ]
    x = split(jnp.concatenate(inputs, axis=0))
    x = split(dot3((block_ref[0], block_ref[1]), x, NN))
    x = dot3(x, (radial1_ref[0], radial1_ref[1]), NT).reshape(2, 4, points, width)
    for i, slot in enumerate((0, 1, jnp.maximum(count - 2, 0), jnp.maximum(count - 1, 0))):
        for part in range(2):
            local_ref[part, slot] = local_ref[part, slot] + x[part, i]
    wide = 2 * slots
    traces = [
        jnp.concatenate(
            [local_ref[part, s, point : point + 1] for part in range(2) for s in range(slots)], axis=0
        )
        for point in (points - 1, 0)
    ]
    corners = jnp.concatenate(
        [
            jnp.broadcast_to(axial_ref[1, i : i + 1, j : j + 1], (1, width))
            for i in (points - 1, 0)
            for j in (0, points - 1)
        ]
        + [jnp.zeros((4, width), F32)],
        axis=0,
    )
    for to in range(message_ref.shape[0]):
        message_ref[to, 0:wide] = traces[0]
        message_ref[to, wide : 2 * wide] = traces[1]
        message_ref[to, 2 * wide : 3 * wide] = ends_ref[0]
        message_ref[to, 3 * wide : 4 * wide] = ends_ref[1]
        message_ref[to, 4 * wide :] = corners


def project_kernel(
    sub_of,
    inverse,
    info_ref,
    received_ref,
    mask_ref,
    axial_ref,
    basis_ref,
    gram_ref,
    before_ref,
    w_ref,
    sums_ref,
    rows_ref,
):
    krylov, _, slots, points, width = basis_ref.shape
    subs = received_ref.shape[0]
    wide = 2 * slots
    count = info_ref[0]
    sub = sub_of()
    after = [received_ref[s, 2 * wide : 3 * wide] for s in range(subs)]
    before = [received_ref[s, 3 * wide : 4 * wide] for s in range(subs)]
    tops = []
    bottoms = []
    for s in range(subs):
        top = received_ref[s, 0:wide]
        bottom = received_ref[s, wide : 2 * wide]
        corner = received_ref[s, 4 * wide :]
        if s > 0:
            top = top + PENALTY * corner[0:1] * after[s - 1]
            bottom = bottom + PENALTY * corner[2:3] * after[s - 1]
        if s < subs - 1:
            top = top + PENALTY * corner[1:2] * before[s + 1]
            bottom = bottom + PENALTY * corner[3:4] * before[s + 1]
        tops.append(top)
        bottoms.append(bottom)
    jumps = [(tops[j - 1] - bottoms[j]) * mask_ref[...] for j in range(1, subs)]

    def solved(at):
        g = jnp.zeros((wide, width), F32)
        for j in range(subs - 1):
            weight = F32(0.0)
            for i in range(subs - 1):
                weight = jnp.where(at == i + 1, F32(inverse[i, j]), weight)
            g = g + weight * jumps[j]
        return g

    def spread(i, x):
        for row in range(wide):
            rows_ref[i, row] = jnp.broadcast_to(x[row : row + 1], (8, width))

    spread(0, solved(sub))
    spread(1, -solved(sub + 1))
    previous = jnp.zeros((wide, width), F32)
    following = jnp.zeros((wide, width), F32)
    for s in range(subs):
        previous = jnp.where(sub == s + 1, PENALTY * after[s], previous)
        following = jnp.where(sub == s - 1, PENALTY * before[s], following)
    spread(2, previous)
    spread(3, following)

    position = lax.broadcasted_iota(jnp.int32, (points, 128), 0).astype(F32) / (points - 1)
    weights = [
        1.0 - position,
        position,
        jnp.broadcast_to(axial_ref[1, :, 0:1], (points, 128)),
        jnp.broadcast_to(axial_ref[1, :, points - 1 : points], (points, 128)),
    ]

    def step(slot, sums):
        sums = list(sums)
        for c in range(0, width, 128):
            rows = [
                [rows_ref[i, part * slots + slot, :, c : c + 128] for i in range(4)]
                for part in range(2)
            ]
            for r in range(0, points, 8):
                w = []
                for part in range(2):
                    x = before_ref[part, slot, r : r + 8, c : c + 128]
                    for i in range(4):
                        x = x + weights[i][r : r + 8] * rows[part][i]
                    w_ref[part, slot, r : r + 8, c : c + 128] = x
                    w.append(x)
                for k in range(krylov):
                    q = [basis_ref[k, part, slot, r : r + 8, c : c + 128] for part in range(2)]
                    sums[2 * k] = sums[2 * k] + (q[0] * w[0] + q[1] * w[1])
                    sums[2 * k + 1] = sums[2 * k + 1] + (q[0] * w[1] - q[1] * w[0])
                sums[2 * krylov] = sums[2 * krylov] + (w[0] * w[0] + w[1] * w[1])
        return tuple(sums)

    sums = lax.fori_loop(
        0, count, step, tuple(jnp.zeros((8, 128), F32) for _ in range(2 * krylov + 1))
    )
    lane = lax.broadcasted_iota(jnp.int32, (1, 128), 1)
    out = gram_ref[...]
    for i, s in enumerate(sums):
        out = out + jnp.where(lane == i, jnp.sum(s, keepdims=True), 0.0)
    for to in range(sums_ref.shape[0]):
        sums_ref[to] = out


def finish_kernel(dof, info_ref, sums_ref, basis_ref, w_ref, out_ref, coeffs_ref, norm_ref):
    krylov, _, slots, points, width = basis_ref.shape
    count = info_ref[0]
    total = jnp.sum(sums_ref[...], axis=0) / dof

    def at(i):
        return total[:, i : i + 1]

    re = [at(2 * k) for k in range(krylov)]
    im = [at(2 * k + 1) for k in range(krylov)]
    squares = at(2 * krylov)
    place = 2 * krylov + 1
    for i in range(krylov):
        squares = squares - 2.0 * (re[i] * re[i] + im[i] * im[i])
        for j in range(i, krylov):
            if i == j:
                squares = squares + (re[i] * re[i] + im[i] * im[i]) * at(place)
                place += 1
            else:
                both = (re[i] * re[j] + im[i] * im[j]) * at(place)
                cross = (re[i] * im[j] - im[i] * re[j]) * at(place + 1)
                squares = squares + 2.0 * (both - cross)
                place += 2
    norm = jnp.sqrt(squares + EPSILON)
    norm_ref[...] = norm
    coeffs_ref[...] = jnp.concatenate(
        [jnp.concatenate(re, axis=1), jnp.concatenate(im, axis=1)], axis=0
    )
    scale = jnp.broadcast_to(1.0 / norm, (8, 128))
    re = [jnp.broadcast_to(x, (8, 128)) for x in re]
    im = [jnp.broadcast_to(x, (8, 128)) for x in im]

    def live(slot, carry):
        for r in range(0, points, 8):
            for c in range(0, width, 128):
                rest_re = w_ref[0, slot, r : r + 8, c : c + 128]
                rest_im = w_ref[1, slot, r : r + 8, c : c + 128]
                for k in range(krylov):
                    q = [basis_ref[k, part, slot, r : r + 8, c : c + 128] for part in range(2)]
                    rest_re = rest_re - (re[k] * q[0] - im[k] * q[1])
                    rest_im = rest_im - (re[k] * q[1] + im[k] * q[0])
                out_ref[0, slot, r : r + 8, c : c + 128] = rest_re * scale
                out_ref[1, slot, r : r + 8, c : c + 128] = rest_im * scale
        return carry

    def empty(slot, carry):
        for part in range(2):
            out_ref[part, slot] = jnp.zeros((points, width), F32)
        return carry

    lax.fori_loop(0, count, live, 0)
    lax.fori_loop(count, slots, empty, 0)


def params(mebibytes=24):
    return pltpu.CompilerParams(vmem_limit_bytes=mebibytes * 2**20)


def body(outer, inner, mode_cost, iface_index, basis, radial, axial, flow_coupling, swirl, shift):
    krylov, _, slots, points, width = basis.shape
    modes = mode_cost.shape[0]
    groups = outer * inner
    subs = lax.axis_size("mer")

    def group_of():
        return lax.axis_index("outer") * inner + lax.axis_index("inner")

    def sub_of():
        return lax.axis_index("mer")

    mode = ("outer", "inner")
    shape = jax.ShapeDtypeStruct
    info, to_other, to_pair = pl.pallas_call(
        functools.partial(layout_kernel, group_of, krylov),
        out_shape=(
            shape((2,), jnp.int32),
            shape((2, 2, points, width), F32),
            shape((2, 2, points, width), F32),
        ),
        in_specs=[VMEM, ANY],
        out_specs=(SMEM, VMEM, VMEM),
        scratch_shapes=[pltpu.SemaphoreType.DMA((2, 2))],
        compiler_params=params(52),
        cost_estimate=pl.CostEstimate(flops=10**10, bytes_accessed=2**18, transcendentals=0),
        name="layout",
    )(mode_cost.reshape(-1, math.gcd(modes, 128)), basis)
    other = [(i, i + 1) for i in range(1, groups - 1, 2)]
    other += [(j, i) for i, j in other]
    from_other = lax.ppermute(to_other, mode, other)
    from_pair = lax.ppermute(to_pair, mode, [(i, i ^ 1) for i in range(groups)])

    rows = slots * points
    local, ends, block, radial1, gram, mask = pl.pallas_call(
        functools.partial(inner_kernel, modes),
        out_shape=(
            shape((2, slots, points, width), F32),
            shape((2, 2 * slots, width), F32),
            shape((2, rows, rows), BF16),
            shape((2, width, width), BF16),
            shape((1, 128), F32),
            shape((1, width), F32),
        ),
        in_specs=[SMEM, SMEM, SMEM, VMEM, VMEM, VMEM, VMEM, VMEM],
        out_specs=(VMEM,) * 6,
        scratch_shapes=[pltpu.VMEM((2, rows, width), BF16)] * 2,
        compiler_params=params(),
        cost_estimate=pl.CostEstimate(flops=10**9, bytes_accessed=8 * 2**20, transcendentals=0),
        name="inner",
    )(info, iface_index, shift, basis, radial, axial, flow_coupling, swirl)

    wide = 2 * slots
    local, message = pl.pallas_call(
        functools.partial(halo_kernel, group_of, modes),
        out_shape=(
            shape(local.shape, F32),
            shape((subs, 4 * wide + 8, width), F32),
        ),
        in_specs=[SMEM] + [VMEM] * 8,
        out_specs=(VMEM, VMEM),
        compiler_params=params(),
        name="halo",
    )(info, from_other, from_pair, flow_coupling, block, radial1, ends, axial, local)
    received = lax.all_to_all(message, "mer", 0, 0)

    system = np.diag(np.full(subs - 1, SCHUR_DIAG)) - np.eye(subs - 1, k=1) - np.eye(subs - 1, k=-1)
    w, sums = pl.pallas_call(
        functools.partial(project_kernel, sub_of, np.linalg.inv(system)),
        out_shape=(shape(local.shape, F32), shape((inner, 1, 128), F32)),
        in_specs=[SMEM] + [VMEM] * 6,
        out_specs=(VMEM, VMEM),
        scratch_shapes=[pltpu.VMEM((4, wide, 8, width), F32)],
        compiler_params=params(),
        name="project",
    )(info, received, mask, axial, basis, gram, local)

    sums = lax.all_to_all(sums, "inner", 0, 0)
    sums = jnp.broadcast_to(jnp.sum(sums, axis=0, keepdims=True), (outer * subs, 1, 128))
    sums = lax.all_to_all(sums, ("outer", "mer"), 0, 0)

    new_vector, coeffs, norm = pl.pallas_call(
        functools.partial(finish_kernel, float(modes * points * subs * width)),
        out_shape=(shape(local.shape, F32), shape((2, krylov), F32), shape((1, 1), F32)),
        in_specs=[SMEM] + [VMEM] * 3,
        compiler_params=params(),
        name="finish",
    )(info, sums, basis, w)
    return new_vector, coeffs, norm.reshape(())


def solution(mesh):
    groups, subs = mesh.devices.shape
    inner = math.gcd(16, groups // 2)
    outer = groups // inner
    fine = Mesh(mesh.devices.reshape(outer, inner, subs), ("outer", "inner", "mer"))
    mode = ("outer", "inner")
    in_specs = (
        P(),
        P(),
        P(None, None, mode, "mer", None),
        P(),
        P(None, "mer", None),
        P(None, "mer", None),
        P("mer", None),
        P(),
    )
    out_specs = (P(None, mode, "mer", None), P(), P())
    return jax.shard_map(
        functools.partial(body, outer, inner),
        mesh=fine,
        in_specs=in_specs,
        out_specs=out_specs,
        check_vma=False,
    )
```

```python
import functools
import math

import jax
import jax.numpy as jnp
import numpy as np
from jax import lax
from jax.experimental import pallas as pl
from jax.experimental.pallas import tpu as pltpu
from jax.sharding import Mesh
from jax.sharding import PartitionSpec as P

QUOTA = 840
PENALTY = 1.0
SCHUR_DIAG = 2.2
EPSILON = 1e-06

VMEM = pl.BlockSpec(memory_space=pltpu.VMEM)
ANY = pl.BlockSpec(memory_space=pl.ANY)
SMEM = pl.BlockSpec(memory_space=pltpu.SMEM)
F32 = jnp.float32
BF16 = jnp.bfloat16
NT = (((1,), (1,)), ((), ()))
NN = (((1,), (0,)), ((), ()))


def split(x):
    high = x.astype(BF16)
    return high, (x - high.astype(F32)).astype(BF16)


def dot3(a, b, dims):
    along = dims[0][1][0]
    left = jnp.concatenate([a[0], a[0], a[1]], axis=1)
    right = jnp.concatenate([b[0], b[1], b[0]], axis=along)
    return lax.dot_general(left, right, dims, preferred_element_type=F32)


def block_diagonal(block, copies):
    n = block.shape[0]
    size = n * copies
    rows = lax.broadcasted_iota(jnp.int32, (n, size), 0)
    cols = lax.broadcasted_iota(jnp.int32, (n, size), 1)
    spread = jnp.where(cols % n == rows, 1.0, 0.0).astype(BF16)
    on = (
        lax.broadcasted_iota(jnp.int32, (size, size), 0) // n
        == lax.broadcasted_iota(jnp.int32, (size, size), 1) // n
    )
    parts = []
    for part in split(block):
        tiled = lax.dot_general(part, spread, NN, preferred_element_type=F32)
        tiled = jnp.concatenate([tiled] * copies, axis=0)
        parts.append(jnp.where(on, tiled, 0.0).astype(BF16))
    return parts


def layout_kernel(group_of, krylov, cost_ref, basis_ref, info_ref, other_ref, pair_ref, sems):
    group = group_of()
    even = lax.rem(group, 2) == 0

    def copy(at, ref, which, part):
        return pltpu.make_async_copy(
            basis_ref.at[krylov - 1, part, pl.ds(at, 2)], ref.at[part], sems.at[which, part]
        )

    @pl.when(even)
    def _():
        for part in range(2):
            copy(0, other_ref, 0, part).start()

    @pl.when(jnp.logical_not(even))
    def _():
        for part in range(2):
            copy(0, pair_ref, 0, part).start()

    cost = cost_ref[...]
    rows, lanes = cost.shape
    lane = lax.broadcasted_iota(jnp.int32, cost.shape, 1)
    row = lax.broadcasted_iota(jnp.int32, cost.shape, 0)
    total = cost
    step = 1
    while step < lanes:
        total = total + jnp.where(lane >= step, pltpu.roll(total, step, 1), 0)
        step *= 2
    prefix = total - cost
    for i in range(rows - 1):
        prefix = prefix + jnp.where(row > i, total[i : i + 1, lanes - 1 :], 0)
    base = 2 * rows * lanes
    both = jnp.where(prefix < group * QUOTA, 1.0, 0.0)
    both = both + jnp.where(prefix < (group + 1) * QUOTA, float(base), 0.0)
    both = jnp.sum(both).astype(jnp.int32)
    start = lax.rem(both, base)
    count = lax.div(both, base) - start

    top = jnp.maximum(count - 2, 0)

    @pl.when(even)
    def _():
        for part in range(2):
            copy(top, pair_ref, 1, part).start()

    @pl.when(jnp.logical_not(even))
    def _():
        for part in range(2):
            copy(top, other_ref, 1, part).start()

    info_ref[0] = count
    info_ref[1] = start
    for which in range(2):
        for part in range(2):
            copy(0, pair_ref, which, part).wait()


def inner_kernel(
    modes,
    info_ref,
    iface_ref,
    shift_ref,
    basis_ref,
    radial_ref,
    axial_ref,
    flow_ref,
    swirl_ref,
    local_ref,
    ends_ref,
    block_ref,
    radial1_ref,
    gram_ref,
    mask_ref,
    high_ref,
    low_ref,
):
    krylov, _, slots, points, width = basis_ref.shape
    count = info_ref[0]
    start = info_ref[1]
    rows = slots * points
    last = krylov - 1

    pairs = [(i, j) for i in range(krylov) for j in range(i, krylov)]
    n_sums = sum(1 if i == j else 2 for i, j in pairs)

    def gram_step(slot, sums):
        sums = list(sums)
        for r in range(0, points, 8):
            for c in range(0, width, 128):
                q = [
                    [basis_ref[k, p, slot, r : r + 8, c : c + 128] for p in range(2)]
                    for k in range(krylov)
                ]
                at = 0
                for i, j in pairs:
                    sums[at] = sums[at] + (q[i][0] * q[j][0] + q[i][1] * q[j][1])
                    at += 1
                    if i != j:
                        sums[at] = sums[at] + (q[i][0] * q[j][1] - q[i][1] * q[j][0])
                        at += 1
        return tuple(sums)

    sums = lax.fori_loop(0, count, gram_step, tuple(jnp.zeros((8, 128), F32) for _ in range(n_sums)))
    lane = lax.broadcasted_iota(jnp.int32, (1, 128), 1)
    gram = jnp.zeros((1, 128), F32)
    for i, s in enumerate(sums):
        gram = gram + jnp.where(lane == 2 * krylov + 1 + i, jnp.sum(s, keepdims=True), 0.0)
    gram_ref[...] = gram

    chosen = iface_ref[...].astype(F32)
    chosen = jnp.broadcast_to(chosen, (chosen.shape[1], chosen.shape[1])).T
    for c in range(0, width, chosen.shape[1]):
        column = lax.broadcasted_iota(jnp.int32, chosen.shape, 1) + c
        hits = jnp.where(chosen == column.astype(F32), 1.0, 0.0)
        mask_ref[:, c : c + chosen.shape[1]] = jnp.sum(hits, axis=0, keepdims=True)

    first_block = block_diagonal(axial_ref[0], slots)
    second_block = block_diagonal(axial_ref[1], slots)
    block_ref[0] = second_block[0]
    block_ref[1] = second_block[1]
    radial1 = split(radial_ref[1])
    radial1_ref[0] = radial1[0]
    radial1_ref[1] = radial1[1]
    radial0 = split(radial_ref[0])


    def current(part, slot):
        return jnp.where(slot < count, basis_ref[last, part, slot], 0.0)

    for part in range(2):
        for slot in range(slots):
            high, low = split(current(part, slot))
            high_ref[part, slot * points : (slot + 1) * points] = high
            low_ref[part, slot * points : (slot + 1) * points] = low

    for part in range(2):
        v = (high_ref[part], low_ref[part])
        image = dot3(v, radial0, NT) + dot3(first_block, v, NN)
        local_ref[part] = image.reshape(slots, points, width)

    for which, point in enumerate((points - 1, 0)):
        picked = jnp.concatenate(
            [
                jnp.where(s < count, basis_ref[last, part, s, point : point + 1], 0.0)
                for part in range(2)
                for s in range(slots)
            ],
            axis=0,
        )
        ends_ref[which] = dot3(split(picked), radial1, NT)

    sigma_re = shift_ref[0]
    sigma_im = shift_ref[1]
    for slot in range(slots):
        wave = (start + slot).astype(F32) / modes
        rotation = wave * swirl_ref[...]
        turn = rotation - sigma_im
        v_re = current(0, slot)
        v_im = current(1, slot)
        new = [
            local_ref[0, slot] - turn * v_im - sigma_re * v_re,
            local_ref[1, slot] + turn * v_re - sigma_re * v_im,
        ]
        for which, offset in enumerate((-2, -1, 1, 2)):
            if 0 <= slot + offset < slots:
                for part in range(2):
                    new[part] = new[part] + flow_ref[which] * current(part, slot + offset)
        for part in range(2):
            high, low = split(jnp.where(slot < count, new[part], 0.0))
            high_ref[part, slot * points : (slot + 1) * points] = high
            low_ref[part, slot * points : (slot + 1) * points] = low

    for part in range(2):
        x = (high_ref[part], low_ref[part])
        x = split(dot3(second_block, x, NN))
        local_ref[part] = dot3(x, radial1, NT).reshape(slots, points, width)


def halo_kernel(
    group_of,
    modes,
    info_ref,
    other_ref,
    pair_ref,
    flow_ref,
    block_ref,
    radial1_ref,
    ends_ref,
    axial_ref,
    before_ref,
    local_ref,
    message_ref,
):
    _, slots, points, width = local_ref.shape
    local_ref[...] = before_ref[...]
    count = info_ref[0]
    end = count + info_ref[1]
    group = group_of()
    even = lax.rem(group, 2) == 0
    inputs = []
    for part in range(2):
        lower = [jnp.where(even, other_ref[part, i], pair_ref[part, i]) for i in range(2)]
        upper = [jnp.where(even, pair_ref[part, i], other_ref[part, i]) for i in range(2)]
        lower = [jnp.where(group > 0, x, 0.0) for x in lower]
        upper = [jnp.where(end + i < modes, x, 0.0) for i, x in enumerate(upper)]
        inputs += [
            jnp.where(count > 0, flow_ref[0] * lower[0] + flow_ref[1] * lower[1], 0.0),
            jnp.where(count > 1, flow_ref[0] * lower[1], 0.0),
            flow_ref[3] * upper[0],
            flow_ref[2] * upper[0] + flow_ref[3] * upper[1],
        ]
    x = split(jnp.concatenate(inputs, axis=0))
    x = split(dot3((block_ref[0], block_ref[1]), x, NN))
    x = dot3(x, (radial1_ref[0], radial1_ref[1]), NT).reshape(2, 4, points, width)
    for i, slot in enumerate((0, 1, jnp.maximum(count - 2, 0), jnp.maximum(count - 1, 0))):
        for part in range(2):
            local_ref[part, slot] = local_ref[part, slot] + x[part, i]
    wide = 2 * slots
    traces = [
        jnp.concatenate(
            [local_ref[part, s, point : point + 1] for part in range(2) for s in range(slots)], axis=0
        )
        for point in (points - 1, 0)
    ]
    corners = jnp.concatenate(
        [
            jnp.broadcast_to(axial_ref[1, i : i + 1, j : j + 1], (1, width))
            for i in (points - 1, 0)
            for j in (0, points - 1)
        ]
        + [jnp.zeros((4, width), F32)],
        axis=0,
    )
    for to in range(message_ref.shape[0]):
        message_ref[to, 0:wide] = traces[0]
        message_ref[to, wide : 2 * wide] = traces[1]
        message_ref[to, 2 * wide : 3 * wide] = ends_ref[0]
        message_ref[to, 3 * wide : 4 * wide] = ends_ref[1]
        message_ref[to, 4 * wide :] = corners


def project_kernel(
    sub_of,
    inverse,
    info_ref,
    received_ref,
    mask_ref,
    axial_ref,
    basis_ref,
    gram_ref,
    before_ref,
    w_ref,
    sums_ref,
    rows_ref,
):
    krylov, _, slots, points, width = basis_ref.shape
    subs = received_ref.shape[0]
    wide = 2 * slots
    count = info_ref[0]
    sub = sub_of()
    after = [received_ref[s, 2 * wide : 3 * wide] for s in range(subs)]
    before = [received_ref[s, 3 * wide : 4 * wide] for s in range(subs)]
    tops = []
    bottoms = []
    for s in range(subs):
        top = received_ref[s, 0:wide]
        bottom = received_ref[s, wide : 2 * wide]
        corner = received_ref[s, 4 * wide :]
        if s > 0:
            top = top + PENALTY * corner[0:1] * after[s - 1]
            bottom = bottom + PENALTY * corner[2:3] * after[s - 1]
        if s < subs - 1:
            top = top + PENALTY * corner[1:2] * before[s + 1]
            bottom = bottom + PENALTY * corner[3:4] * before[s + 1]
        tops.append(top)
        bottoms.append(bottom)
    jumps = [(tops[j - 1] - bottoms[j]) * mask_ref[...] for j in range(1, subs)]

    def solved(at):
        g = jnp.zeros((wide, width), F32)
        for j in range(subs - 1):
            weight = F32(0.0)
            for i in range(subs - 1):
                weight = jnp.where(at == i + 1, F32(inverse[i, j]), weight)
            g = g + weight * jumps[j]
        return g

    def spread(i, x):
        for row in range(wide):
            rows_ref[i, row] = jnp.broadcast_to(x[row : row + 1], (8, width))

    spread(0, solved(sub))
    spread(1, -solved(sub + 1))
    previous = jnp.zeros((wide, width), F32)
    following = jnp.zeros((wide, width), F32)
    for s in range(subs):
        previous = jnp.where(sub == s + 1, PENALTY * after[s], previous)
        following = jnp.where(sub == s - 1, PENALTY * before[s], following)
    spread(2, previous)
    spread(3, following)

    position = lax.broadcasted_iota(jnp.int32, (points, 128), 0).astype(F32) / (points - 1)
    weights = [
        1.0 - position,
        position,
        jnp.broadcast_to(axial_ref[1, :, 0:1], (points, 128)),
        jnp.broadcast_to(axial_ref[1, :, points - 1 : points], (points, 128)),
    ]

    def step(slot, sums):
        sums = list(sums)
        for c in range(0, width, 128):
            rows = [
                [rows_ref[i, part * slots + slot, :, c : c + 128] for i in range(4)]
                for part in range(2)
            ]
            for r in range(0, points, 8):
                w = []
                for part in range(2):
                    x = before_ref[part, slot, r : r + 8, c : c + 128]
                    for i in range(4):
                        x = x + weights[i][r : r + 8] * rows[part][i]
                    w_ref[part, slot, r : r + 8, c : c + 128] = x
                    w.append(x)
                for k in range(krylov):
                    q = [basis_ref[k, part, slot, r : r + 8, c : c + 128] for part in range(2)]
                    sums[2 * k] = sums[2 * k] + (q[0] * w[0] + q[1] * w[1])
                    sums[2 * k + 1] = sums[2 * k + 1] + (q[0] * w[1] - q[1] * w[0])
                sums[2 * krylov] = sums[2 * krylov] + (w[0] * w[0] + w[1] * w[1])
        return tuple(sums)

    sums = lax.fori_loop(
        0, count, step, tuple(jnp.zeros((8, 128), F32) for _ in range(2 * krylov + 1))
    )
    lane = lax.broadcasted_iota(jnp.int32, (1, 128), 1)
    out = gram_ref[...]
    for i, s in enumerate(sums):
        out = out + jnp.where(lane == i, jnp.sum(s, keepdims=True), 0.0)
    for to in range(sums_ref.shape[0]):
        sums_ref[to] = out


def finish_kernel(dof, info_ref, sums_ref, basis_ref, w_ref, out_ref, coeffs_ref, norm_ref):
    krylov, _, slots, points, width = basis_ref.shape
    count = info_ref[0]
    total = jnp.sum(sums_ref[...], axis=0) / dof

    def at(i):
        return total[:, i : i + 1]

    re = [at(2 * k) for k in range(krylov)]
    im = [at(2 * k + 1) for k in range(krylov)]
    squares = at(2 * krylov)
    place = 2 * krylov + 1
    for i in range(krylov):
        squares = squares - 2.0 * (re[i] * re[i] + im[i] * im[i])
        for j in range(i, krylov):
            if i == j:
                squares = squares + (re[i] * re[i] + im[i] * im[i]) * at(place)
                place += 1
            else:
                both = (re[i] * re[j] + im[i] * im[j]) * at(place)
                cross = (re[i] * im[j] - im[i] * re[j]) * at(place + 1)
                squares = squares + 2.0 * (both - cross)
                place += 2
    norm = jnp.sqrt(squares + EPSILON)
    norm_ref[...] = norm
    coeffs_ref[...] = jnp.concatenate(
        [jnp.concatenate(re, axis=1), jnp.concatenate(im, axis=1)], axis=0
    )
    scale = jnp.broadcast_to(1.0 / norm, (8, 128))
    re = [jnp.broadcast_to(x, (8, 128)) for x in re]
    im = [jnp.broadcast_to(x, (8, 128)) for x in im]

    def live(slot, carry):
        for r in range(0, points, 8):
            for c in range(0, width, 128):
                rest_re = w_ref[0, slot, r : r + 8, c : c + 128]
                rest_im = w_ref[1, slot, r : r + 8, c : c + 128]
                for k in range(krylov):
                    q = [basis_ref[k, part, slot, r : r + 8, c : c + 128] for part in range(2)]
                    rest_re = rest_re - (re[k] * q[0] - im[k] * q[1])
                    rest_im = rest_im - (re[k] * q[1] + im[k] * q[0])
                out_ref[0, slot, r : r + 8, c : c + 128] = rest_re * scale
                out_ref[1, slot, r : r + 8, c : c + 128] = rest_im * scale
        return carry

    def empty(slot, carry):
        for part in range(2):
            out_ref[part, slot] = jnp.zeros((points, width), F32)
        return carry

    lax.fori_loop(0, count, live, 0)
    lax.fori_loop(count, slots, empty, 0)


def params(mebibytes=24):
    return pltpu.CompilerParams(vmem_limit_bytes=mebibytes * 2**20)


def body(outer, inner, mode_cost, iface_index, basis, radial, axial, flow_coupling, swirl, shift):
    krylov, _, slots, points, width = basis.shape
    modes = mode_cost.shape[0]
    groups = outer * inner
    subs = lax.axis_size("mer")

    def group_of():
        return lax.axis_index("outer") * inner + lax.axis_index("inner")

    def sub_of():
        return lax.axis_index("mer")

    mode = ("outer", "inner")
    shape = jax.ShapeDtypeStruct
    info, to_other, to_pair = pl.pallas_call(
        functools.partial(layout_kernel, group_of, krylov),
        out_shape=(
            shape((2,), jnp.int32),
            shape((2, 2, points, width), F32),
            shape((2, 2, points, width), F32),
        ),
        in_specs=[VMEM, ANY],
        out_specs=(SMEM, VMEM, VMEM),
        scratch_shapes=[pltpu.SemaphoreType.DMA((2, 2))],
        compiler_params=params(52),
        cost_estimate=pl.CostEstimate(flops=10**10, bytes_accessed=2**18, transcendentals=0),
        name="layout",
    )(mode_cost.reshape(-1, math.gcd(modes, 128)), basis)
    other = [(i, i + 1) for i in range(1, groups - 1, 2)]
    other += [(j, i) for i, j in other]
    from_other = lax.ppermute(to_other, mode, other)
    from_pair = lax.ppermute(to_pair, mode, [(i, i ^ 1) for i in range(groups)])

    rows = slots * points
    local, ends, block, radial1, gram, mask = pl.pallas_call(
        functools.partial(inner_kernel, modes),
        out_shape=(
            shape((2, slots, points, width), F32),
            shape((2, 2 * slots, width), F32),
            shape((2, rows, rows), BF16),
            shape((2, width, width), BF16),
            shape((1, 128), F32),
            shape((1, width), F32),
        ),
        in_specs=[SMEM, VMEM, SMEM, VMEM, VMEM, VMEM, VMEM, VMEM],
        out_specs=(VMEM,) * 6,
        scratch_shapes=[pltpu.VMEM((2, rows, width), BF16)] * 2,
        compiler_params=params(),
        cost_estimate=pl.CostEstimate(flops=10**9, bytes_accessed=8 * 2**20, transcendentals=0),
        name="inner",
    )(info, iface_index.reshape(1, -1), shift, basis, radial, axial, flow_coupling, swirl)

    wide = 2 * slots
    local, message = pl.pallas_call(
        functools.partial(halo_kernel, group_of, modes),
        out_shape=(
            shape(local.shape, F32),
            shape((subs, 4 * wide + 8, width), F32),
        ),
        in_specs=[SMEM] + [VMEM] * 8,
        out_specs=(VMEM, VMEM),
        compiler_params=params(),
        name="halo",
    )(info, from_other, from_pair, flow_coupling, block, radial1, ends, axial, local)
    received = lax.all_to_all(message, "mer", 0, 0)

    system = np.diag(np.full(subs - 1, SCHUR_DIAG)) - np.eye(subs - 1, k=1) - np.eye(subs - 1, k=-1)
    w, sums = pl.pallas_call(
        functools.partial(project_kernel, sub_of, np.linalg.inv(system)),
        out_shape=(shape(local.shape, F32), shape((inner, 1, 128), F32)),
        in_specs=[SMEM] + [VMEM] * 6,
        out_specs=(VMEM, VMEM),
        scratch_shapes=[pltpu.VMEM((4, wide, 8, width), F32)],
        compiler_params=params(),
        name="project",
    )(info, received, mask, axial, basis, gram, local)

    sums = lax.all_to_all(sums, "inner", 0, 0)
    sums = jnp.broadcast_to(jnp.sum(sums, axis=0, keepdims=True), (outer * subs, 1, 128))
    sums = lax.all_to_all(sums, ("outer", "mer"), 0, 0)

    new_vector, coeffs, norm = pl.pallas_call(
        functools.partial(finish_kernel, float(modes * points * subs * width)),
        out_shape=(shape(local.shape, F32), shape((2, krylov), F32), shape((1, 1), F32)),
        in_specs=[SMEM] + [VMEM] * 3,
        compiler_params=params(),
        name="finish",
    )(info, sums, basis, w)
    return new_vector, coeffs, norm.reshape(())


def solution(mesh):
    groups, subs = mesh.devices.shape
    inner = math.gcd(16, groups // 2)
    outer = groups // inner
    fine = Mesh(mesh.devices.reshape(outer, inner, subs), ("outer", "inner", "mer"))
    mode = ("outer", "inner")
    in_specs = (
        P(),
        P(),
        P(None, None, mode, "mer", None),
        P(),
        P(None, "mer", None),
        P(None, "mer", None),
        P("mer", None),
        P(),
    )
    out_specs = (P(None, mode, "mer", None), P(), P())
    return jax.shard_map(
        functools.partial(body, outer, inner),
        mesh=fine,
        in_specs=in_specs,
        out_specs=out_specs,
        check_vma=False,
    )
```

```python
import functools
import math

import jax
import jax.numpy as jnp
import numpy as np
from jax import lax
from jax.experimental import pallas as pl
from jax.experimental.pallas import tpu as pltpu
from jax.sharding import Mesh
from jax.sharding import PartitionSpec as P

QUOTA = 840
PENALTY = 1.0
SCHUR_DIAG = 2.2
EPSILON = 1e-06

VMEM = pl.BlockSpec(memory_space=pltpu.VMEM)
ANY = pl.BlockSpec(memory_space=pl.ANY)
SMEM = pl.BlockSpec(memory_space=pltpu.SMEM)
F32 = jnp.float32
BF16 = jnp.bfloat16
NT = (((1,), (1,)), ((), ()))
NN = (((1,), (0,)), ((), ()))


def split(x):
    high = x.astype(BF16)
    return high, (x - high.astype(F32)).astype(BF16)


def dot3(a, b, dims):
    along = dims[0][1][0]
    left = jnp.concatenate([a[0], a[0], a[1]], axis=1)
    right = jnp.concatenate([b[0], b[1], b[0]], axis=along)
    return lax.dot_general(left, right, dims, preferred_element_type=F32)


def block_diagonal(block, copies):
    n = block.shape[0]
    size = n * copies
    rows = lax.broadcasted_iota(jnp.int32, (n, size), 0)
    cols = lax.broadcasted_iota(jnp.int32, (n, size), 1)
    spread = jnp.where(cols % n == rows, 1.0, 0.0).astype(BF16)
    on = (
        lax.broadcasted_iota(jnp.int32, (size, size), 0) // n
        == lax.broadcasted_iota(jnp.int32, (size, size), 1) // n
    )
    parts = []
    for part in split(block):
        tiled = lax.dot_general(part, spread, NN, preferred_element_type=F32)
        tiled = jnp.concatenate([tiled] * copies, axis=0)
        parts.append(jnp.where(on, tiled, 0.0).astype(BF16))
    return parts


def layout_kernel(group_of, krylov, cost_ref, basis_ref, info_ref, other_ref, pair_ref, vector_ref, sem):
    group = group_of()
    even = lax.rem(group, 2) == 0
    fetch = pltpu.make_async_copy(basis_ref.at[krylov - 1], vector_ref, sem)
    fetch.start()

    cost = cost_ref[...]
    rows, lanes = cost.shape
    lane = lax.broadcasted_iota(jnp.int32, cost.shape, 1)
    row = lax.broadcasted_iota(jnp.int32, cost.shape, 0)
    total = cost
    step = 1
    while step < lanes:
        total = total + jnp.where(lane >= step, pltpu.roll(total, step, 1), 0)
        step *= 2
    prefix = total - cost
    for i in range(rows - 1):
        prefix = prefix + jnp.where(row > i, total[i : i + 1, lanes - 1 :], 0)
    base = 2 * rows * lanes
    both = jnp.where(prefix < group * QUOTA, 1.0, 0.0)
    both = both + jnp.where(prefix < (group + 1) * QUOTA, float(base), 0.0)
    both = jnp.sum(both).astype(jnp.int32)
    start = lax.rem(both, base)
    count = lax.div(both, base) - start

    info_ref[0] = count
    info_ref[1] = start
    top = jnp.maximum(count - 2, 0)
    to_pair = jnp.where(even, top, 0)
    to_other = jnp.where(even, 0, top)
    fetch.wait()
    for part in range(2):
        for i in range(2):
            other_ref[part, i] = vector_ref[part, to_other + i]
            pair_ref[part, i] = vector_ref[part, to_pair + i]


def inner_kernel(
    modes,
    info_ref,
    iface_ref,
    shift_ref,
    basis_ref,
    radial_ref,
    axial_ref,
    flow_ref,
    swirl_ref,
    local_ref,
    ends_ref,
    block_ref,
    radial1_ref,
    gram_ref,
    mask_ref,
    high_ref,
    low_ref,
):
    krylov, _, slots, points, width = basis_ref.shape
    count = info_ref[0]
    start = info_ref[1]
    rows = slots * points
    last = krylov - 1

    pairs = [(i, j) for i in range(krylov) for j in range(i, krylov)]
    n_sums = sum(1 if i == j else 2 for i, j in pairs)

    def gram_step(slot, sums):
        sums = list(sums)
        for r in range(0, points, 8):
            for c in range(0, width, 128):
                q = [
                    [basis_ref[k, p, slot, r : r + 8, c : c + 128] for p in range(2)]
                    for k in range(krylov)
                ]
                at = 0
                for i, j in pairs:
                    sums[at] = sums[at] + (q[i][0] * q[j][0] + q[i][1] * q[j][1])
                    at += 1
                    if i != j:
                        sums[at] = sums[at] + (q[i][0] * q[j][1] - q[i][1] * q[j][0])
                        at += 1
        return tuple(sums)

    sums = lax.fori_loop(0, count, gram_step, tuple(jnp.zeros((8, 128), F32) for _ in range(n_sums)))
    lane = lax.broadcasted_iota(jnp.int32, (1, 128), 1)
    gram = jnp.zeros((1, 128), F32)
    for i, s in enumerate(sums):
        gram = gram + jnp.where(lane == 2 * krylov + 1 + i, jnp.sum(s, keepdims=True), 0.0)
    gram_ref[...] = gram

    chosen = iface_ref[...].astype(F32)
    chosen = jnp.broadcast_to(chosen, (chosen.shape[1], chosen.shape[1])).T
    for c in range(0, width, chosen.shape[1]):
        column = lax.broadcasted_iota(jnp.int32, chosen.shape, 1) + c
        hits = jnp.where(chosen == column.astype(F32), 1.0, 0.0)
        mask_ref[:, c : c + chosen.shape[1]] = jnp.sum(hits, axis=0, keepdims=True)

    first_block = block_diagonal(axial_ref[0], slots)
    second_block = block_diagonal(axial_ref[1], slots)
    block_ref[0] = second_block[0]
    block_ref[1] = second_block[1]
    radial1 = split(radial_ref[1])
    radial1_ref[0] = radial1[0]
    radial1_ref[1] = radial1[1]
    radial0 = split(radial_ref[0])


    def current(part, slot):
        return jnp.where(slot < count, basis_ref[last, part, slot], 0.0)

    for part in range(2):
        for slot in range(slots):
            high, low = split(current(part, slot))
            high_ref[part, slot * points : (slot + 1) * points] = high
            low_ref[part, slot * points : (slot + 1) * points] = low

    for part in range(2):
        v = (high_ref[part], low_ref[part])
        image = dot3(v, radial0, NT) + dot3(first_block, v, NN)
        local_ref[part] = image.reshape(slots, points, width)

    for which, point in enumerate((points - 1, 0)):
        picked = jnp.concatenate(
            [
                jnp.where(s < count, basis_ref[last, part, s, point : point + 1], 0.0)
                for part in range(2)
                for s in range(slots)
            ],
            axis=0,
        )
        ends_ref[which] = dot3(split(picked), radial1, NT)

    sigma_re = shift_ref[0]
    sigma_im = shift_ref[1]
    for slot in range(slots):
        wave = (start + slot).astype(F32) / modes
        rotation = wave * swirl_ref[...]
        turn = rotation - sigma_im
        v_re = current(0, slot)
        v_im = current(1, slot)
        new = [
            local_ref[0, slot] - turn * v_im - sigma_re * v_re,
            local_ref[1, slot] + turn * v_re - sigma_re * v_im,
        ]
        for which, offset in enumerate((-2, -1, 1, 2)):
            if 0 <= slot + offset < slots:
                for part in range(2):
                    new[part] = new[part] + flow_ref[which] * current(part, slot + offset)
        for part in range(2):
            high, low = split(jnp.where(slot < count, new[part], 0.0))
            high_ref[part, slot * points : (slot + 1) * points] = high
            low_ref[part, slot * points : (slot + 1) * points] = low

    for part in range(2):
        x = (high_ref[part], low_ref[part])
        x = split(dot3(second_block, x, NN))
        local_ref[part] = dot3(x, radial1, NT).reshape(slots, points, width)


def halo_kernel(
    group_of,
    modes,
    info_ref,
    other_ref,
    pair_ref,
    flow_ref,
    block_ref,
    radial1_ref,
    ends_ref,
    axial_ref,
    before_ref,
    local_ref,
    message_ref,
):
    _, slots, points, width = local_ref.shape
    local_ref[...] = before_ref[...]
    count = info_ref[0]
    end = count + info_ref[1]
    group = group_of()
    even = lax.rem(group, 2) == 0
    inputs = []
    for part in range(2):
        lower = [jnp.where(even, other_ref[part, i], pair_ref[part, i]) for i in range(2)]
        upper = [jnp.where(even, pair_ref[part, i], other_ref[part, i]) for i in range(2)]
        lower = [jnp.where(group > 0, x, 0.0) for x in lower]
        upper = [jnp.where(end + i < modes, x, 0.0) for i, x in enumerate(upper)]
        inputs += [
            jnp.where(count > 0, flow_ref[0] * lower[0] + flow_ref[1] * lower[1], 0.0),
            jnp.where(count > 1, flow_ref[0] * lower[1], 0.0),
            flow_ref[3] * upper[0],
            flow_ref[2] * upper[0] + flow_ref[3] * upper[1],
        ]
    x = split(jnp.concatenate(inputs, axis=0))
    x = split(dot3((block_ref[0], block_ref[1]), x, NN))
    x = dot3(x, (radial1_ref[0], radial1_ref[1]), NT).reshape(2, 4, points, width)
    for i, slot in enumerate((0, 1, jnp.maximum(count - 2, 0), jnp.maximum(count - 1, 0))):
        for part in range(2):
            local_ref[part, slot] = local_ref[part, slot] + x[part, i]
    wide = 2 * slots
    traces = [
        jnp.concatenate(
            [local_ref[part, s, point : point + 1] for part in range(2) for s in range(slots)], axis=0
        )
        for point in (points - 1, 0)
    ]
    corners = jnp.concatenate(
        [
            jnp.broadcast_to(axial_ref[1, i : i + 1, j : j + 1], (1, width))
            for i in (points - 1, 0)
            for j in (0, points - 1)
        ]
        + [jnp.zeros((4, width), F32)],
        axis=0,
    )
    for to in range(message_ref.shape[0]):
        message_ref[to, 0:wide] = traces[0]
        message_ref[to, wide : 2 * wide] = traces[1]
        message_ref[to, 2 * wide : 3 * wide] = ends_ref[0]
        message_ref[to, 3 * wide : 4 * wide] = ends_ref[1]
        message_ref[to, 4 * wide :] = corners


def project_kernel(
    sub_of,
    inverse,
    info_ref,
    received_ref,
    mask_ref,
    axial_ref,
    basis_ref,
    gram_ref,
    before_ref,
    w_ref,
    sums_ref,
    rows_ref,
):
    krylov, _, slots, points, width = basis_ref.shape
    subs = received_ref.shape[0]
    wide = 2 * slots
    count = info_ref[0]
    sub = sub_of()
    after = [received_ref[s, 2 * wide : 3 * wide] for s in range(subs)]
    before = [received_ref[s, 3 * wide : 4 * wide] for s in range(subs)]
    tops = []
    bottoms = []
    for s in range(subs):
        top = received_ref[s, 0:wide]
        bottom = received_ref[s, wide : 2 * wide]
        corner = received_ref[s, 4 * wide :]
        if s > 0:
            top = top + PENALTY * corner[0:1] * after[s - 1]
            bottom = bottom + PENALTY * corner[2:3] * after[s - 1]
        if s < subs - 1:
            top = top + PENALTY * corner[1:2] * before[s + 1]
            bottom = bottom + PENALTY * corner[3:4] * before[s + 1]
        tops.append(top)
        bottoms.append(bottom)
    jumps = [(tops[j - 1] - bottoms[j]) * mask_ref[...] for j in range(1, subs)]

    def solved(at):
        g = jnp.zeros((wide, width), F32)
        for j in range(subs - 1):
            weight = F32(0.0)
            for i in range(subs - 1):
                weight = jnp.where(at == i + 1, F32(inverse[i, j]), weight)
            g = g + weight * jumps[j]
        return g

    def spread(i, x):
        for row in range(wide):
            rows_ref[i, row] = jnp.broadcast_to(x[row : row + 1], (8, width))

    spread(0, solved(sub))
    spread(1, -solved(sub + 1))
    previous = jnp.zeros((wide, width), F32)
    following = jnp.zeros((wide, width), F32)
    for s in range(subs):
        previous = jnp.where(sub == s + 1, PENALTY * after[s], previous)
        following = jnp.where(sub == s - 1, PENALTY * before[s], following)
    spread(2, previous)
    spread(3, following)

    position = lax.broadcasted_iota(jnp.int32, (points, 128), 0).astype(F32) / (points - 1)
    weights = [
        1.0 - position,
        position,
        jnp.broadcast_to(axial_ref[1, :, 0:1], (points, 128)),
        jnp.broadcast_to(axial_ref[1, :, points - 1 : points], (points, 128)),
    ]

    def step(slot, sums):
        sums = list(sums)
        for c in range(0, width, 128):
            rows = [
                [rows_ref[i, part * slots + slot, :, c : c + 128] for i in range(4)]
                for part in range(2)
            ]
            for r in range(0, points, 8):
                w = []
                for part in range(2):
                    x = before_ref[part, slot, r : r + 8, c : c + 128]
                    for i in range(4):
                        x = x + weights[i][r : r + 8] * rows[part][i]
                    w_ref[part, slot, r : r + 8, c : c + 128] = x
                    w.append(x)
                for k in range(krylov):
                    q = [basis_ref[k, part, slot, r : r + 8, c : c + 128] for part in range(2)]
                    sums[2 * k] = sums[2 * k] + (q[0] * w[0] + q[1] * w[1])
                    sums[2 * k + 1] = sums[2 * k + 1] + (q[0] * w[1] - q[1] * w[0])
                sums[2 * krylov] = sums[2 * krylov] + (w[0] * w[0] + w[1] * w[1])
        return tuple(sums)

    sums = lax.fori_loop(
        0, count, step, tuple(jnp.zeros((8, 128), F32) for _ in range(2 * krylov + 1))
    )
    lane = lax.broadcasted_iota(jnp.int32, (1, 128), 1)
    out = gram_ref[...]
    order = [i // 2 + krylov * (i % 2) for i in range(2 * krylov)] + [2 * krylov]
    for i, s in zip(order, sums):
        out = out + jnp.where(lane == i, jnp.sum(s, keepdims=True), 0.0)
    for to in range(sums_ref.shape[0]):
        sums_ref[to] = out


def finish_kernel(dof, info_ref, sums_ref, basis_ref, w_ref, out_ref, coeffs_ref, norm_ref):
    krylov, _, slots, points, width = basis_ref.shape
    count = info_ref[0]
    total = jnp.sum(sums_ref[...], axis=0) / dof

    def at(i):
        return total[:, i : i + 1]

    re = [at(k) for k in range(krylov)]
    im = [at(krylov + k) for k in range(krylov)]
    squares = at(2 * krylov)
    place = 2 * krylov + 1
    for i in range(krylov):
        squares = squares - 2.0 * (re[i] * re[i] + im[i] * im[i])
        for j in range(i, krylov):
            if i == j:
                squares = squares + (re[i] * re[i] + im[i] * im[i]) * at(place)
                place += 1
            else:
                both = (re[i] * re[j] + im[i] * im[j]) * at(place)
                cross = (re[i] * im[j] - im[i] * re[j]) * at(place + 1)
                squares = squares + 2.0 * (both - cross)
                place += 2
    norm = jnp.sqrt(squares + EPSILON)
    norm_ref[...] = norm
    coeffs_ref[0:1] = total[:, 0:krylov]
    coeffs_ref[1:2] = total[:, krylov : 2 * krylov]
    scale = jnp.broadcast_to(1.0 / norm, (8, 128))
    re = [jnp.broadcast_to(x, (8, 128)) for x in re]
    im = [jnp.broadcast_to(x, (8, 128)) for x in im]

    def live(slot, carry):
        for r in range(0, points, 8):
            for c in range(0, width, 128):
                rest_re = w_ref[0, slot, r : r + 8, c : c + 128]
                rest_im = w_ref[1, slot, r : r + 8, c : c + 128]
                for k in range(krylov):
                    q = [basis_ref[k, part, slot, r : r + 8, c : c + 128] for part in range(2)]
                    rest_re = rest_re - (re[k] * q[0] - im[k] * q[1])
                    rest_im = rest_im - (re[k] * q[1] + im[k] * q[0])
                out_ref[0, slot, r : r + 8, c : c + 128] = rest_re * scale
                out_ref[1, slot, r : r + 8, c : c + 128] = rest_im * scale
        return carry

    def empty(slot, carry):
        for part in range(2):
            out_ref[part, slot] = jnp.zeros((points, width), F32)
        return carry

    lax.fori_loop(0, count, live, 0)
    lax.fori_loop(count, slots, empty, 0)


def params(mebibytes=24):
    return pltpu.CompilerParams(vmem_limit_bytes=mebibytes * 2**20)


def body(outer, inner, mode_cost, iface_index, basis, radial, axial, flow_coupling, swirl, shift):
    krylov, _, slots, points, width = basis.shape
    modes = mode_cost.shape[0]
    groups = outer * inner
    subs = lax.axis_size("mer")

    def group_of():
        return lax.axis_index("outer") * inner + lax.axis_index("inner")

    def sub_of():
        return lax.axis_index("mer")

    mode = ("outer", "inner")
    shape = jax.ShapeDtypeStruct
    info, to_other, to_pair = pl.pallas_call(
        functools.partial(layout_kernel, group_of, krylov),
        out_shape=(
            shape((2,), jnp.int32),
            shape((2, 2, points, width), F32),
            shape((2, 2, points, width), F32),
        ),
        in_specs=[VMEM, ANY],
        out_specs=(SMEM, VMEM, VMEM),
        scratch_shapes=[pltpu.VMEM((2, slots, points, width), F32), pltpu.SemaphoreType.DMA],
        compiler_params=params(52),
        cost_estimate=pl.CostEstimate(flops=10**10, bytes_accessed=2**18, transcendentals=0),
        name="layout",
    )(mode_cost.reshape(-1, math.gcd(modes, 128)), basis)
    other = [(i, i + 1) for i in range(1, groups - 1, 2)]
    other += [(j, i) for i, j in other]
    from_other = lax.ppermute(to_other, mode, other)
    from_pair = lax.ppermute(to_pair, mode, [(i, i ^ 1) for i in range(groups)])

    rows = slots * points
    local, ends, block, radial1, gram, mask = pl.pallas_call(
        functools.partial(inner_kernel, modes),
        out_shape=(
            shape((2, slots, points, width), F32),
            shape((2, 2 * slots, width), F32),
            shape((2, rows, rows), BF16),
            shape((2, width, width), BF16),
            shape((1, 128), F32),
            shape((1, width), F32),
        ),
        in_specs=[SMEM, VMEM, SMEM, VMEM, VMEM, VMEM, VMEM, VMEM],
        out_specs=(VMEM,) * 6,
        scratch_shapes=[pltpu.VMEM((2, rows, width), BF16)] * 2,
        compiler_params=params(),
        cost_estimate=pl.CostEstimate(flops=10**9, bytes_accessed=8 * 2**20, transcendentals=0),
        name="inner",
    )(info, iface_index.reshape(1, -1), shift, basis, radial, axial, flow_coupling, swirl)

    wide = 2 * slots
    local, message = pl.pallas_call(
        functools.partial(halo_kernel, group_of, modes),
        out_shape=(
            shape(local.shape, F32),
            shape((subs, 4 * wide + 8, width), F32),
        ),
        in_specs=[SMEM] + [VMEM] * 8,
        out_specs=(VMEM, VMEM),
        compiler_params=params(),
        name="halo",
    )(info, from_other, from_pair, flow_coupling, block, radial1, ends, axial, local)
    received = lax.all_to_all(message, "mer", 0, 0)

    system = np.diag(np.full(subs - 1, SCHUR_DIAG)) - np.eye(subs - 1, k=1) - np.eye(subs - 1, k=-1)
    w, sums = pl.pallas_call(
        functools.partial(project_kernel, sub_of, np.linalg.inv(system)),
        out_shape=(shape(local.shape, F32), shape((inner, 1, 128), F32)),
        in_specs=[SMEM] + [VMEM] * 6,
        out_specs=(VMEM, VMEM),
        scratch_shapes=[pltpu.VMEM((4, wide, 8, width), F32)],
        compiler_params=params(),
        name="project",
    )(info, received, mask, axial, basis, gram, local)

    sums = lax.all_to_all(sums, "inner", 0, 0)
    sums = jnp.broadcast_to(jnp.sum(sums, axis=0, keepdims=True), (outer * subs, 1, 128))
    sums = lax.all_to_all(sums, ("outer", "mer"), 0, 0)

    new_vector, coeffs, norm = pl.pallas_call(
        functools.partial(finish_kernel, float(modes * points * subs * width)),
        out_shape=(shape(local.shape, F32), shape((2, krylov), F32), shape((1, 1), F32)),
        in_specs=[SMEM] + [VMEM] * 3,
        compiler_params=params(),
        name="finish",
    )(info, sums, basis, w)
    return new_vector, coeffs, norm.reshape(())


def solution(mesh):
    groups, subs = mesh.devices.shape
    inner = math.gcd(16, groups // 2)
    outer = groups // inner
    fine = Mesh(mesh.devices.reshape(outer, inner, subs), ("outer", "inner", "mer"))
    mode = ("outer", "inner")
    in_specs = (
        P(),
        P(),
        P(None, None, mode, "mer", None),
        P(),
        P(None, "mer", None),
        P(None, "mer", None),
        P("mer", None),
        P(),
    )
    out_specs = (P(None, mode, "mer", None), P(), P())
    return jax.shard_map(
        functools.partial(body, outer, inner),
        mesh=fine,
        in_specs=in_specs,
        out_specs=out_specs,
        check_vma=False,
    )
```

```python
import functools
import math

import jax
import jax.numpy as jnp
import numpy as np
from jax import lax
from jax.experimental import pallas as pl
from jax.experimental.pallas import tpu as pltpu
from jax.sharding import Mesh
from jax.sharding import PartitionSpec as P

QUOTA = 840
PENALTY = 1.0
SCHUR_DIAG = 2.2
EPSILON = 1e-06

VMEM = pl.BlockSpec(memory_space=pltpu.VMEM)
ANY = pl.BlockSpec(memory_space=pl.ANY)
SMEM = pl.BlockSpec(memory_space=pltpu.SMEM)
F32 = jnp.float32
BF16 = jnp.bfloat16
NT = (((1,), (1,)), ((), ()))
NN = (((1,), (0,)), ((), ()))


def split(x):
    high = x.astype(BF16)
    return high, (x - high.astype(F32)).astype(BF16)


def dot3(a, b, dims):
    along = dims[0][1][0]
    left = jnp.concatenate([a[0], a[0], a[1]], axis=1)
    right = jnp.concatenate([b[0], b[1], b[0]], axis=along)
    return lax.dot_general(left, right, dims, preferred_element_type=F32)


def block_diagonal(block, copies):
    n = block.shape[0]
    size = n * copies
    rows = lax.broadcasted_iota(jnp.int32, (n, size), 0)
    cols = lax.broadcasted_iota(jnp.int32, (n, size), 1)
    spread = jnp.where(cols % n == rows, 1.0, 0.0).astype(BF16)
    on = (
        lax.broadcasted_iota(jnp.int32, (size, size), 0) // n
        == lax.broadcasted_iota(jnp.int32, (size, size), 1) // n
    )
    parts = []
    for part in split(block):
        tiled = lax.dot_general(part, spread, NN, preferred_element_type=F32)
        tiled = jnp.concatenate([tiled] * copies, axis=0)
        parts.append(jnp.where(on, tiled, 0.0).astype(BF16))
    return parts


def layout_kernel(group_of, krylov, cost_ref, basis_ref, info_ref, other_ref, pair_ref, sems):
    group = group_of()
    even = lax.rem(group, 2) == 0

    def copy(at, ref, which, part):
        return pltpu.make_async_copy(
            basis_ref.at[krylov - 1, part, pl.ds(at, 2)], ref.at[part], sems.at[which, part]
        )

    @pl.when(even)
    def _():
        for part in range(2):
            copy(0, other_ref, 0, part).start()

    @pl.when(jnp.logical_not(even))
    def _():
        for part in range(2):
            copy(0, pair_ref, 0, part).start()

    cost = cost_ref[...]
    rows, lanes = cost.shape
    lane = lax.broadcasted_iota(jnp.int32, cost.shape, 1)
    row = lax.broadcasted_iota(jnp.int32, cost.shape, 0)
    total = cost
    step = 1
    while step < lanes:
        total = total + jnp.where(lane >= step, pltpu.roll(total, step, 1), 0)
        step *= 2
    prefix = total - cost
    for i in range(rows - 1):
        prefix = prefix + jnp.where(row > i, total[i : i + 1, lanes - 1 :], 0)
    base = 2 * rows * lanes
    both = jnp.where(prefix < group * QUOTA, 1.0, 0.0)
    both = both + jnp.where(prefix < (group + 1) * QUOTA, float(base), 0.0)
    both = jnp.sum(both).astype(jnp.int32)
    start = lax.rem(both, base)
    count = lax.div(both, base) - start

    top = jnp.maximum(count - 2, 0)

    @pl.when(even)
    def _():
        for part in range(2):
            copy(top, pair_ref, 1, part).start()

    @pl.when(jnp.logical_not(even))
    def _():
        for part in range(2):
            copy(top, other_ref, 1, part).start()

    info_ref[0] = count
    info_ref[1] = start
    for which in range(2):
        for part in range(2):
            copy(0, pair_ref, which, part).wait()


def inner_kernel(
    modes,
    info_ref,
    iface_ref,
    shift_ref,
    basis_ref,
    radial_ref,
    axial_ref,
    flow_ref,
    swirl_ref,
    local_ref,
    ends_ref,
    block_ref,
    radial1_ref,
    gram_ref,
    mask_ref,
    high_ref,
    low_ref,
):
    krylov, _, slots, points, width = basis_ref.shape
    count = info_ref[0]
    start = info_ref[1]
    rows = slots * points
    last = krylov - 1

    pairs = [(i, j) for i in range(krylov) for j in range(i, krylov)]
    n_sums = sum(1 if i == j else 2 for i, j in pairs)

    def gram_step(slot, sums):
        sums = list(sums)
        for r in range(0, points, 8):
            for c in range(0, width, 128):
                q = [
                    [basis_ref[k, p, slot, r : r + 8, c : c + 128] for p in range(2)]
                    for k in range(krylov)
                ]
                at = 0
                for i, j in pairs:
                    sums[at] = sums[at] + (q[i][0] * q[j][0] + q[i][1] * q[j][1])
                    at += 1
                    if i != j:
                        sums[at] = sums[at] + (q[i][0] * q[j][1] - q[i][1] * q[j][0])
                        at += 1
        return tuple(sums)

    sums = lax.fori_loop(0, count, gram_step, tuple(jnp.zeros((8, 128), F32) for _ in range(n_sums)))
    lane = lax.broadcasted_iota(jnp.int32, (1, 128), 1)
    gram = jnp.zeros((1, 128), F32)
    for i, s in enumerate(sums):
        gram = gram + jnp.where(lane == 2 * krylov + 1 + i, jnp.sum(s, keepdims=True), 0.0)
    gram_ref[...] = gram

    chosen = iface_ref[...].astype(F32)
    chosen = jnp.broadcast_to(chosen, (chosen.shape[1], chosen.shape[1])).T
    for c in range(0, width, chosen.shape[1]):
        column = lax.broadcasted_iota(jnp.int32, chosen.shape, 1) + c
        hits = jnp.where(chosen == column.astype(F32), 1.0, 0.0)
        mask_ref[:, c : c + chosen.shape[1]] = jnp.sum(hits, axis=0, keepdims=True)

    first_block = block_diagonal(axial_ref[0], slots)
    second_block = block_diagonal(axial_ref[1], slots)
    block_ref[0] = second_block[0]
    block_ref[1] = second_block[1]
    radial1 = split(radial_ref[1])
    radial1_ref[0] = radial1[0]
    radial1_ref[1] = radial1[1]
    radial0 = split(radial_ref[0])


    def current(part, slot):
        return jnp.where(slot < count, basis_ref[last, part, slot], 0.0)

    for part in range(2):
        for slot in range(slots):
            high, low = split(current(part, slot))
            high_ref[part, slot * points : (slot + 1) * points] = high
            low_ref[part, slot * points : (slot + 1) * points] = low

    for part in range(2):
        v = (high_ref[part], low_ref[part])
        image = dot3(v, radial0, NT) + dot3(first_block, v, NN)
        local_ref[part] = image.reshape(slots, points, width)

    for which, point in enumerate((points - 1, 0)):
        picked = jnp.concatenate(
            [
                jnp.where(s < count, basis_ref[last, part, s, point : point + 1], 0.0)
                for part in range(2)
                for s in range(slots)
            ],
            axis=0,
        )
        ends_ref[which] = dot3(split(picked), radial1, NT)

    sigma_re = shift_ref[0]
    sigma_im = shift_ref[1]
    for slot in range(slots):
        wave = (start + slot).astype(F32) / modes
        rotation = wave * swirl_ref[...]
        turn = rotation - sigma_im
        v_re = current(0, slot)
        v_im = current(1, slot)
        new = [
            local_ref[0, slot] - turn * v_im - sigma_re * v_re,
            local_ref[1, slot] + turn * v_re - sigma_re * v_im,
        ]
        for which, offset in enumerate((-2, -1, 1, 2)):
            if 0 <= slot + offset < slots:
                for part in range(2):
                    new[part] = new[part] + flow_ref[which] * current(part, slot + offset)
        for part in range(2):
            high, low = split(jnp.where(slot < count, new[part], 0.0))
            high_ref[part, slot * points : (slot + 1) * points] = high
            low_ref[part, slot * points : (slot + 1) * points] = low

    for part in range(2):
        x = (high_ref[part], low_ref[part])
        x = split(dot3(second_block, x, NN))
        local_ref[part] = dot3(x, radial1, NT).reshape(slots, points, width)


def halo_kernel(
    group_of,
    modes,
    info_ref,
    other_ref,
    pair_ref,
    flow_ref,
    block_ref,
    radial1_ref,
    ends_ref,
    axial_ref,
    mask_ref,
    before_ref,
    local_ref,
    message_ref,
):
    _, slots, points, width = local_ref.shape
    local_ref[...] = before_ref[...]
    count = info_ref[0]
    end = count + info_ref[1]
    group = group_of()
    even = lax.rem(group, 2) == 0
    inputs = []
    for part in range(2):
        lower = [jnp.where(even, other_ref[part, i], pair_ref[part, i]) for i in range(2)]
        upper = [jnp.where(even, pair_ref[part, i], other_ref[part, i]) for i in range(2)]
        lower = [jnp.where(group > 0, x, 0.0) for x in lower]
        upper = [jnp.where(end + i < modes, x, 0.0) for i, x in enumerate(upper)]
        inputs += [
            jnp.where(count > 0, flow_ref[0] * lower[0] + flow_ref[1] * lower[1], 0.0),
            jnp.where(count > 1, flow_ref[0] * lower[1], 0.0),
            flow_ref[3] * upper[0],
            flow_ref[2] * upper[0] + flow_ref[3] * upper[1],
        ]
    x = split(jnp.concatenate(inputs, axis=0))
    x = split(dot3((block_ref[0], block_ref[1]), x, NN))
    x = dot3(x, (radial1_ref[0], radial1_ref[1]), NT).reshape(2, 4, points, width)
    for i, slot in enumerate((0, 1, jnp.maximum(count - 2, 0), jnp.maximum(count - 1, 0))):
        for part in range(2):
            local_ref[part, slot] = local_ref[part, slot] + x[part, i]
    wide = 2 * slots
    traces = [
        jnp.concatenate(
            [local_ref[part, s, point : point + 1] for part in range(2) for s in range(slots)], axis=0
        )
        for point in (points - 1, 0)
    ]
    corners = jnp.concatenate(
        [
            jnp.broadcast_to(axial_ref[1, i : i + 1, j : j + 1], (1, width))
            for i in (points - 1, 0)
            for j in (0, points - 1)
        ]
        + [jnp.zeros((wide - 4, width), F32)],
        axis=0,
    )
    top = jnp.where(mask_ref[...] > 0.0, traces[0], corners)
    for to in range(message_ref.shape[0]):
        message_ref[to, 0:wide] = top
        message_ref[to, wide : 2 * wide] = traces[1]
        message_ref[to, 2 * wide : 3 * wide] = ends_ref[0]
        message_ref[to, 3 * wide : 4 * wide] = ends_ref[1]


def project_kernel(
    sub_of,
    inverse,
    free,
    info_ref,
    received_ref,
    mask_ref,
    axial_ref,
    basis_ref,
    gram_ref,
    before_ref,
    w_ref,
    sums_ref,
    rows_ref,
):
    krylov, _, slots, points, width = basis_ref.shape
    subs = received_ref.shape[0]
    wide = 2 * slots
    count = info_ref[0]
    sub = sub_of()
    chosen = mask_ref[...] > 0.0
    after = [received_ref[s, 2 * wide : 3 * wide] for s in range(subs)]
    before = [received_ref[s, 3 * wide : 4 * wide] for s in range(subs)]
    tops = []
    bottoms = []
    for s in range(subs):
        top = received_ref[s, 0:wide]
        bottom = received_ref[s, wide : 2 * wide]
        corner = jnp.sum(jnp.where(chosen, 0.0, top[0:8]), axis=1, keepdims=True) / free
        if s > 0:
            top = top + PENALTY * corner[0:1] * after[s - 1]
            bottom = bottom + PENALTY * corner[2:3] * after[s - 1]
        if s < subs - 1:
            top = top + PENALTY * corner[1:2] * before[s + 1]
            bottom = bottom + PENALTY * corner[3:4] * before[s + 1]
        tops.append(top)
        bottoms.append(bottom)
    jumps = [jnp.where(chosen, tops[j - 1] - bottoms[j], 0.0) for j in range(1, subs)]

    def solved(at):
        g = jnp.zeros((wide, width), F32)
        for j in range(subs - 1):
            weight = F32(0.0)
            for i in range(subs - 1):
                weight = jnp.where(at == i + 1, F32(inverse[i, j]), weight)
            g = g + weight * jumps[j]
        return g

    def spread(i, x):
        for row in range(wide):
            rows_ref[i, row] = jnp.broadcast_to(x[row : row + 1], (8, width))

    spread(0, solved(sub))
    spread(1, -solved(sub + 1))
    previous = jnp.zeros((wide, width), F32)
    following = jnp.zeros((wide, width), F32)
    for s in range(subs):
        previous = jnp.where(sub == s + 1, PENALTY * after[s], previous)
        following = jnp.where(sub == s - 1, PENALTY * before[s], following)
    spread(2, previous)
    spread(3, following)

    position = lax.broadcasted_iota(jnp.int32, (points, 128), 0).astype(F32) / (points - 1)
    weights = [
        1.0 - position,
        position,
        jnp.broadcast_to(axial_ref[1, :, 0:1], (points, 128)),
        jnp.broadcast_to(axial_ref[1, :, points - 1 : points], (points, 128)),
    ]

    def step(slot, sums):
        sums = list(sums)
        for c in range(0, width, 128):
            rows = [
                [rows_ref[i, part * slots + slot, :, c : c + 128] for i in range(4)]
                for part in range(2)
            ]
            for r in range(0, points, 8):
                w = []
                for part in range(2):
                    x = before_ref[part, slot, r : r + 8, c : c + 128]
                    for i in range(4):
                        x = x + weights[i][r : r + 8] * rows[part][i]
                    w_ref[part, slot, r : r + 8, c : c + 128] = x
                    w.append(x)
                for k in range(krylov):
                    q = [basis_ref[k, part, slot, r : r + 8, c : c + 128] for part in range(2)]
                    sums[2 * k] = sums[2 * k] + (q[0] * w[0] + q[1] * w[1])
                    sums[2 * k + 1] = sums[2 * k + 1] + (q[0] * w[1] - q[1] * w[0])
                sums[2 * krylov] = sums[2 * krylov] + (w[0] * w[0] + w[1] * w[1])
        return tuple(sums)

    sums = lax.fori_loop(
        0, count, step, tuple(jnp.zeros((8, 128), F32) for _ in range(2 * krylov + 1))
    )
    lane = lax.broadcasted_iota(jnp.int32, (1, 128), 1)
    out = gram_ref[...]
    for i, s in enumerate(sums):
        out = out + jnp.where(lane == i, jnp.sum(s, keepdims=True), 0.0)
    for to in range(sums_ref.shape[0]):
        sums_ref[to] = out


def finish_kernel(dof, info_ref, sums_ref, basis_ref, w_ref, out_ref, coeffs_ref, norm_ref):
    krylov, _, slots, points, width = basis_ref.shape
    count = info_ref[0]
    total = jnp.sum(sums_ref[...], axis=0) / dof

    def at(i):
        return total[:, i : i + 1]

    re = [at(2 * k) for k in range(krylov)]
    im = [at(2 * k + 1) for k in range(krylov)]
    squares = at(2 * krylov)
    place = 2 * krylov + 1
    for i in range(krylov):
        squares = squares - 2.0 * (re[i] * re[i] + im[i] * im[i])
        for j in range(i, krylov):
            if i == j:
                squares = squares + (re[i] * re[i] + im[i] * im[i]) * at(place)
                place += 1
            else:
                both = (re[i] * re[j] + im[i] * im[j]) * at(place)
                cross = (re[i] * im[j] - im[i] * re[j]) * at(place + 1)
                squares = squares + 2.0 * (both - cross)
                place += 2
    norm = jnp.sqrt(squares + EPSILON)
    norm_ref[...] = norm
    coeffs_ref[...] = jnp.concatenate(
        [jnp.concatenate(re, axis=1), jnp.concatenate(im, axis=1)], axis=0
    )
    scale = jnp.broadcast_to(1.0 / norm, (8, 128))
    re = [jnp.broadcast_to(x, (8, 128)) for x in re]
    im = [jnp.broadcast_to(x, (8, 128)) for x in im]

    def live(slot, carry):
        for r in range(0, points, 8):
            for c in range(0, width, 128):
                rest_re = w_ref[0, slot, r : r + 8, c : c + 128]
                rest_im = w_ref[1, slot, r : r + 8, c : c + 128]
                for k in range(krylov):
                    q = [basis_ref[k, part, slot, r : r + 8, c : c + 128] for part in range(2)]
                    rest_re = rest_re - (re[k] * q[0] - im[k] * q[1])
                    rest_im = rest_im - (re[k] * q[1] + im[k] * q[0])
                out_ref[0, slot, r : r + 8, c : c + 128] = rest_re * scale
                out_ref[1, slot, r : r + 8, c : c + 128] = rest_im * scale
        return carry

    def empty(slot, carry):
        for part in range(2):
            out_ref[part, slot] = jnp.zeros((points, width), F32)
        return carry

    lax.fori_loop(0, count, live, 0)
    lax.fori_loop(count, slots, empty, 0)


def params(mebibytes=24):
    return pltpu.CompilerParams(vmem_limit_bytes=mebibytes * 2**20)


def body(outer, inner, mode_cost, iface_index, basis, radial, axial, flow_coupling, swirl, shift):
    krylov, _, slots, points, width = basis.shape
    modes = mode_cost.shape[0]
    groups = outer * inner
    subs = lax.axis_size("mer")

    def group_of():
        return lax.axis_index("outer") * inner + lax.axis_index("inner")

    def sub_of():
        return lax.axis_index("mer")

    mode = ("outer", "inner")
    shape = jax.ShapeDtypeStruct
    info, to_other, to_pair = pl.pallas_call(
        functools.partial(layout_kernel, group_of, krylov),
        out_shape=(
            shape((2,), jnp.int32),
            shape((2, 2, points, width), F32),
            shape((2, 2, points, width), F32),
        ),
        in_specs=[VMEM, ANY],
        out_specs=(SMEM, VMEM, VMEM),
        scratch_shapes=[pltpu.SemaphoreType.DMA((2, 2))],
        compiler_params=params(52),
        cost_estimate=pl.CostEstimate(flops=10**10, bytes_accessed=2**18, transcendentals=0),
        name="layout",
    )(mode_cost.reshape(-1, math.gcd(modes, 128)), basis)
    other = [(i, i + 1) for i in range(1, groups - 1, 2)]
    other += [(j, i) for i, j in other]
    from_other = lax.ppermute(to_other, mode, other)
    from_pair = lax.ppermute(to_pair, mode, [(i, i ^ 1) for i in range(groups)])

    rows = slots * points
    local, ends, block, radial1, gram, mask = pl.pallas_call(
        functools.partial(inner_kernel, modes),
        out_shape=(
            shape((2, slots, points, width), F32),
            shape((2, 2 * slots, width), F32),
            shape((2, rows, rows), BF16),
            shape((2, width, width), BF16),
            shape((1, 128), F32),
            shape((1, width), F32),
        ),
        in_specs=[SMEM, VMEM, SMEM, VMEM, VMEM, VMEM, VMEM, VMEM],
        out_specs=(VMEM,) * 6,
        scratch_shapes=[pltpu.VMEM((2, rows, width), BF16)] * 2,
        compiler_params=params(),
        cost_estimate=pl.CostEstimate(flops=10**9, bytes_accessed=8 * 2**20, transcendentals=0),
        name="inner",
    )(info, iface_index.reshape(1, -1), shift, basis, radial, axial, flow_coupling, swirl)

    wide = 2 * slots
    local, message = pl.pallas_call(
        functools.partial(halo_kernel, group_of, modes),
        out_shape=(
            shape(local.shape, F32),
            shape((subs, 4 * wide, width), F32),
        ),
        in_specs=[SMEM] + [VMEM] * 9,
        out_specs=(VMEM, VMEM),
        compiler_params=params(),
        name="halo",
    )(info, from_other, from_pair, flow_coupling, block, radial1, ends, axial, mask, local)
    received = lax.all_to_all(message, "mer", 0, 0)

    system = np.diag(np.full(subs - 1, SCHUR_DIAG)) - np.eye(subs - 1, k=1) - np.eye(subs - 1, k=-1)
    w, sums = pl.pallas_call(
        functools.partial(
            project_kernel, sub_of, np.linalg.inv(system), float(width - iface_index.shape[0])
        ),
        out_shape=(shape(local.shape, F32), shape((inner, 1, 128), F32)),
        in_specs=[SMEM] + [VMEM] * 6,
        out_specs=(VMEM, VMEM),
        scratch_shapes=[pltpu.VMEM((4, wide, 8, width), F32)],
        compiler_params=params(),
        name="project",
    )(info, received, mask, axial, basis, gram, local)

    sums = lax.all_to_all(sums, "inner", 0, 0)
    sums = jnp.broadcast_to(jnp.sum(sums, axis=0, keepdims=True), (outer * subs, 1, 128))
    sums = lax.all_to_all(sums, ("outer", "mer"), 0, 0)

    new_vector, coeffs, norm = pl.pallas_call(
        functools.partial(finish_kernel, float(modes * points * subs * width)),
        out_shape=(shape(local.shape, F32), shape((2, krylov), F32), shape((1, 1), F32)),
        in_specs=[SMEM] + [VMEM] * 3,
        compiler_params=params(),
        name="finish",
    )(info, sums, basis, w)
    return new_vector, coeffs, norm.reshape(())


def solution(mesh):
    groups, subs = mesh.devices.shape
    inner = math.gcd(16, groups // 2)
    outer = groups // inner
    fine = Mesh(mesh.devices.reshape(outer, inner, subs), ("outer", "inner", "mer"))
    mode = ("outer", "inner")
    in_specs = (
        P(),
        P(),
        P(None, None, mode, "mer", None),
        P(),
        P(None, "mer", None),
        P(None, "mer", None),
        P("mer", None),
        P(),
    )
    out_specs = (P(None, mode, "mer", None), P(), P())
    return jax.shard_map(
        functools.partial(body, outer, inner),
        mesh=fine,
        in_specs=in_specs,
        out_specs=out_specs,
        check_vma=False,
    )
```

```python
import functools
import math

import jax
import jax.numpy as jnp
import numpy as np
from jax import lax
from jax.experimental import pallas as pl
from jax.experimental.pallas import tpu as pltpu
from jax.sharding import Mesh
from jax.sharding import PartitionSpec as P

QUOTA = 840
PENALTY = 1.0
SCHUR_DIAG = 2.2
EPSILON = 1e-06

VMEM = pl.BlockSpec(memory_space=pltpu.VMEM)
ANY = pl.BlockSpec(memory_space=pl.ANY)
SMEM = pl.BlockSpec(memory_space=pltpu.SMEM)
F32 = jnp.float32
BF16 = jnp.bfloat16
NT = (((1,), (1,)), ((), ()))
NN = (((1,), (0,)), ((), ()))


def split(x):
    high = x.astype(BF16)
    return high, (x - high.astype(F32)).astype(BF16)


def dot3(a, b, dims):
    along = dims[0][1][0]
    left = jnp.concatenate([a[0], a[0], a[1]], axis=1)
    right = jnp.concatenate([b[0], b[1], b[0]], axis=along)
    return lax.dot_general(left, right, dims, preferred_element_type=F32)


def block_diagonal(block, copies):
    n = block.shape[0]
    size = n * copies
    rows = lax.broadcasted_iota(jnp.int32, (n, size), 0)
    cols = lax.broadcasted_iota(jnp.int32, (n, size), 1)
    spread = jnp.where(cols % n == rows, 1.0, 0.0).astype(BF16)
    on = (
        lax.broadcasted_iota(jnp.int32, (size, size), 0) // n
        == lax.broadcasted_iota(jnp.int32, (size, size), 1) // n
    )
    parts = []
    for part in split(block):
        tiled = lax.dot_general(part, spread, NN, preferred_element_type=F32)
        tiled = jnp.concatenate([tiled] * copies, axis=0)
        parts.append(jnp.where(on, tiled, 0.0).astype(BF16))
    return parts


def layout_kernel(group_of, krylov, cost_ref, basis_ref, info_ref, other_ref, pair_ref, sems):
    group = group_of()
    even = lax.rem(group, 2) == 0

    def copy(at, ref, which, part):
        return pltpu.make_async_copy(
            basis_ref.at[krylov - 1, part, pl.ds(at, 2)], ref.at[part], sems.at[which, part]
        )

    @pl.when(even)
    def _():
        for part in range(2):
            copy(0, other_ref, 0, part).start()

    @pl.when(jnp.logical_not(even))
    def _():
        for part in range(2):
            copy(0, pair_ref, 0, part).start()

    cost = cost_ref[...]
    rows, lanes = cost.shape
    lane = lax.broadcasted_iota(jnp.int32, cost.shape, 1)
    row = lax.broadcasted_iota(jnp.int32, cost.shape, 0)
    total = cost
    step = 1
    while step < lanes:
        total = total + jnp.where(lane >= step, pltpu.roll(total, step, 1), 0)
        step *= 2
    prefix = total - cost
    for i in range(rows - 1):
        prefix = prefix + jnp.where(row > i, total[i : i + 1, lanes - 1 :], 0)
    base = 2 * rows * lanes
    both = jnp.where(prefix < group * QUOTA, 1.0, 0.0)
    both = both + jnp.where(prefix < (group + 1) * QUOTA, float(base), 0.0)
    both = jnp.sum(both).astype(jnp.int32)
    start = lax.rem(both, base)
    count = lax.div(both, base) - start

    top = jnp.maximum(count - 2, 0)

    @pl.when(even)
    def _():
        for part in range(2):
            copy(top, pair_ref, 1, part).start()

    @pl.when(jnp.logical_not(even))
    def _():
        for part in range(2):
            copy(top, other_ref, 1, part).start()

    info_ref[0] = count
    info_ref[1] = start
    for which in range(2):
        for part in range(2):
            copy(0, pair_ref, which, part).wait()


def inner_kernel(
    modes,
    info_ref,
    iface_ref,
    shift_ref,
    basis_ref,
    radial_ref,
    axial_ref,
    flow_ref,
    swirl_ref,
    local_ref,
    ends_ref,
    block_ref,
    radial1_ref,
    gram_ref,
    mask_ref,
    high_ref,
    low_ref,
):
    krylov, _, slots, points, width = basis_ref.shape
    count = info_ref[0]
    start = info_ref[1]
    rows = slots * points
    last = krylov - 1

    pairs = [(i, j) for i in range(krylov) for j in range(i, krylov)]
    n_sums = sum(1 if i == j else 2 for i, j in pairs)

    def gram_step(slot, sums):
        sums = list(sums)
        for r in range(0, points, 8):
            for c in range(0, width, 128):
                q = [
                    [basis_ref[k, p, slot, r : r + 8, c : c + 128] for p in range(2)]
                    for k in range(krylov)
                ]
                at = 0
                for i, j in pairs:
                    sums[at] = sums[at] + (q[i][0] * q[j][0] + q[i][1] * q[j][1])
                    at += 1
                    if i != j:
                        sums[at] = sums[at] + (q[i][0] * q[j][1] - q[i][1] * q[j][0])
                        at += 1
        return tuple(sums)

    sums = lax.fori_loop(0, count, gram_step, tuple(jnp.zeros((8, 128), F32) for _ in range(n_sums)))
    lane = lax.broadcasted_iota(jnp.int32, (1, 128), 1)
    gram = jnp.zeros((1, 128), F32)
    for i, s in enumerate(sums):
        gram = gram + jnp.where(lane == 2 * krylov + 1 + i, jnp.sum(s, keepdims=True), 0.0)
    gram_ref[...] = gram

    chosen = iface_ref[...].astype(F32)
    chosen = jnp.broadcast_to(chosen, (chosen.shape[1], chosen.shape[1])).T
    for c in range(0, width, chosen.shape[1]):
        column = lax.broadcasted_iota(jnp.int32, chosen.shape, 1) + c
        hits = jnp.where(chosen == column.astype(F32), 1.0, 0.0)
        mask_ref[:, c : c + chosen.shape[1]] = jnp.sum(hits, axis=0, keepdims=True)

    first_block = block_diagonal(axial_ref[0], slots)
    second_block = block_diagonal(axial_ref[1], slots)
    block_ref[0] = second_block[0]
    block_ref[1] = second_block[1]
    radial1 = split(radial_ref[1])
    radial1_ref[0] = radial1[0]
    radial1_ref[1] = radial1[1]
    radial0 = split(radial_ref[0])


    def current(part, slot):
        return jnp.where(slot < count, basis_ref[last, part, slot], 0.0)

    for part in range(2):
        for slot in range(slots):
            high, low = split(current(part, slot))
            high_ref[part, slot * points : (slot + 1) * points] = high
            low_ref[part, slot * points : (slot + 1) * points] = low

    for part in range(2):
        v = (high_ref[part], low_ref[part])
        image = dot3(v, radial0, NT) + dot3(first_block, v, NN)
        local_ref[part] = image.reshape(slots, points, width)

    for which, point in enumerate((points - 1, 0)):
        picked = jnp.concatenate(
            [
                jnp.where(s < count, basis_ref[last, part, s, point : point + 1], 0.0)
                for part in range(2)
                for s in range(slots)
            ],
            axis=0,
        )
        ends_ref[which] = dot3(split(picked), radial1, NT)

    sigma_re = shift_ref[0]
    sigma_im = shift_ref[1]
    for slot in range(slots):
        wave = (start + slot).astype(F32) / modes
        rotation = wave * swirl_ref[...]
        turn = rotation - sigma_im
        v_re = current(0, slot)
        v_im = current(1, slot)
        new = [
            local_ref[0, slot] - turn * v_im - sigma_re * v_re,
            local_ref[1, slot] + turn * v_re - sigma_re * v_im,
        ]
        for which, offset in enumerate((-2, -1, 1, 2)):
            if 0 <= slot + offset < slots:
                for part in range(2):
                    new[part] = new[part] + flow_ref[which] * current(part, slot + offset)
        for part in range(2):
            high, low = split(jnp.where(slot < count, new[part], 0.0))
            high_ref[part, slot * points : (slot + 1) * points] = high
            low_ref[part, slot * points : (slot + 1) * points] = low

    for part in range(2):
        x = (high_ref[part], low_ref[part])
        x = split(dot3(second_block, x, NN))
        local_ref[part] = dot3(x, radial1, NT).reshape(slots, points, width)


def halo_kernel(
    group_of,
    modes,
    info_ref,
    other_ref,
    pair_ref,
    flow_ref,
    block_ref,
    radial1_ref,
    ends_ref,
    axial_ref,
    mask_ref,
    before_ref,
    local_ref,
    message_ref,
):
    _, slots, points, width = local_ref.shape
    local_ref[...] = before_ref[...]
    count = info_ref[0]
    end = count + info_ref[1]
    group = group_of()
    even = lax.rem(group, 2) == 0
    inputs = []
    for part in range(2):
        lower = [jnp.where(even, other_ref[part, i], pair_ref[part, i]) for i in range(2)]
        upper = [jnp.where(even, pair_ref[part, i], other_ref[part, i]) for i in range(2)]
        lower = [jnp.where(group > 0, x, 0.0) for x in lower]
        upper = [jnp.where(end + i < modes, x, 0.0) for i, x in enumerate(upper)]
        inputs += [
            jnp.where(count > 0, flow_ref[0] * lower[0] + flow_ref[1] * lower[1], 0.0),
            jnp.where(count > 1, flow_ref[0] * lower[1], 0.0),
            flow_ref[3] * upper[0],
            flow_ref[2] * upper[0] + flow_ref[3] * upper[1],
        ]
    x = split(jnp.concatenate(inputs, axis=0))
    x = split(dot3((block_ref[0], block_ref[1]), x, NN))
    x = dot3(x, (radial1_ref[0], radial1_ref[1]), NT).reshape(2, 4, points, width)
    for i, slot in enumerate((0, 1, jnp.maximum(count - 2, 0), jnp.maximum(count - 1, 0))):
        for part in range(2):
            local_ref[part, slot] = local_ref[part, slot] + x[part, i]
    wide = 2 * slots
    traces = [
        jnp.concatenate(
            [local_ref[part, s, point : point + 1] for part in range(2) for s in range(slots)], axis=0
        )
        for point in (points - 1, 0)
    ]
    corners = jnp.concatenate(
        [
            jnp.broadcast_to(axial_ref[1, i : i + 1, j : j + 1], (1, width))
            for i in (points - 1, 0)
            for j in (0, points - 1)
        ]
        + [jnp.zeros((wide - 4, width), F32)],
        axis=0,
    )
    top = jnp.where(mask_ref[...] > 0.0, traces[0], corners)
    for to in range(message_ref.shape[0]):
        message_ref[to, 0:wide] = top
        message_ref[to, wide : 2 * wide] = traces[1]
        message_ref[to, 2 * wide : 3 * wide] = ends_ref[0]
        message_ref[to, 3 * wide : 4 * wide] = ends_ref[1]


def project_kernel(
    sub_of,
    inverse,
    free,
    info_ref,
    received_ref,
    mask_ref,
    axial_ref,
    basis_ref,
    gram_ref,
    before_ref,
    w_ref,
    sums_ref,
    rows_ref,
):
    krylov, _, slots, points, width = basis_ref.shape
    subs = received_ref.shape[0]
    wide = 2 * slots
    count = info_ref[0]
    sub = sub_of()
    chosen = mask_ref[...] > 0.0
    after = [received_ref[s, 2 * wide : 3 * wide] for s in range(subs)]
    before = [received_ref[s, 3 * wide : 4 * wide] for s in range(subs)]
    tops = []
    bottoms = []
    for s in range(subs):
        top = received_ref[s, 0:wide]
        bottom = received_ref[s, wide : 2 * wide]
        corner = jnp.sum(jnp.where(chosen, 0.0, top[0:8]), axis=1, keepdims=True) / free
        if s > 0:
            top = top + PENALTY * corner[0:1] * after[s - 1]
            bottom = bottom + PENALTY * corner[2:3] * after[s - 1]
        if s < subs - 1:
            top = top + PENALTY * corner[1:2] * before[s + 1]
            bottom = bottom + PENALTY * corner[3:4] * before[s + 1]
        tops.append(top)
        bottoms.append(bottom)
    jumps = [jnp.where(chosen, tops[j - 1] - bottoms[j], 0.0) for j in range(1, subs)]

    def solved(at):
        g = jnp.zeros((wide, width), F32)
        for j in range(subs - 1):
            weight = F32(0.0)
            for i in range(subs - 1):
                weight = jnp.where(at == i + 1, F32(inverse[i, j]), weight)
            g = g + weight * jumps[j]
        return g

    def spread(i, x):
        for row in range(wide):
            rows_ref[i, row] = jnp.broadcast_to(x[row : row + 1], (8, width))

    spread(0, solved(sub))
    spread(1, -solved(sub + 1))
    previous = jnp.zeros((wide, width), F32)
    following = jnp.zeros((wide, width), F32)
    for s in range(subs):
        previous = jnp.where(sub == s + 1, PENALTY * after[s], previous)
        following = jnp.where(sub == s - 1, PENALTY * before[s], following)
    spread(2, previous)
    spread(3, following)

    position = lax.broadcasted_iota(jnp.int32, (points, 128), 0).astype(F32) / (points - 1)
    weights = [
        1.0 - position,
        position,
        jnp.broadcast_to(axial_ref[1, :, 0:1], (points, 128)),
        jnp.broadcast_to(axial_ref[1, :, points - 1 : points], (points, 128)),
    ]

    def step(slot, sums):
        sums = list(sums)
        for c in range(0, width, 128):
            rows = [
                [rows_ref[i, part * slots + slot, :, c : c + 128] for i in range(4)]
                for part in range(2)
            ]
            for r in range(0, points, 8):
                w = []
                for part in range(2):
                    x = before_ref[part, slot, r : r + 8, c : c + 128]
                    for i in range(4):
                        x = x + weights[i][r : r + 8] * rows[part][i]
                    w_ref[part, slot, r : r + 8, c : c + 128] = x
                    w.append(x)
                for k in range(krylov):
                    q = [basis_ref[k, part, slot, r : r + 8, c : c + 128] for part in range(2)]
                    sums[2 * k] = sums[2 * k] + (q[0] * w[0] + q[1] * w[1])
                    sums[2 * k + 1] = sums[2 * k + 1] + (q[0] * w[1] - q[1] * w[0])
                sums[2 * krylov] = sums[2 * krylov] + (w[0] * w[0] + w[1] * w[1])
        return tuple(sums)

    sums = lax.fori_loop(
        0, count, step, tuple(jnp.zeros((8, 128), F32) for _ in range(2 * krylov + 1))
    )
    lane = lax.broadcasted_iota(jnp.int32, (1, 128), 1)
    out = gram_ref[...]
    for i, s in enumerate(sums):
        out = out + jnp.where(lane == i, jnp.sum(s, keepdims=True), 0.0)
    for to in range(sums_ref.shape[0]):
        sums_ref[to] = out


def finish_kernel(dof, info_ref, sums_ref, basis_ref, w_ref, out_ref, coeffs_ref, norm_ref):
    krylov, _, slots, points, width = basis_ref.shape
    count = info_ref[0]
    total = jnp.sum(sums_ref[...], axis=0) / dof

    def at(i):
        return total[:, i : i + 1]

    re = [at(2 * k) for k in range(krylov)]
    im = [at(2 * k + 1) for k in range(krylov)]
    squares = at(2 * krylov)
    place = 2 * krylov + 1
    for i in range(krylov):
        squares = squares - 2.0 * (re[i] * re[i] + im[i] * im[i])
        for j in range(i, krylov):
            if i == j:
                squares = squares + (re[i] * re[i] + im[i] * im[i]) * at(place)
                place += 1
            else:
                both = (re[i] * re[j] + im[i] * im[j]) * at(place)
                cross = (re[i] * im[j] - im[i] * re[j]) * at(place + 1)
                squares = squares + 2.0 * (both - cross)
                place += 2
    norm = jnp.sqrt(squares + EPSILON)
    norm_ref[...] = norm
    coeffs_ref[...] = jnp.concatenate(
        [jnp.concatenate(re, axis=1), jnp.concatenate(im, axis=1)], axis=0
    )
    scale = jnp.broadcast_to(1.0 / norm, (8, 128))
    re = [jnp.broadcast_to(x, (8, 128)) for x in re]
    im = [jnp.broadcast_to(x, (8, 128)) for x in im]

    def live(slot, carry):
        for r in range(0, points, 8):
            for c in range(0, width, 128):
                rest_re = w_ref[0, slot, r : r + 8, c : c + 128]
                rest_im = w_ref[1, slot, r : r + 8, c : c + 128]
                for k in range(krylov):
                    q = [basis_ref[k, part, slot, r : r + 8, c : c + 128] for part in range(2)]
                    rest_re = rest_re - (re[k] * q[0] - im[k] * q[1])
                    rest_im = rest_im - (re[k] * q[1] + im[k] * q[0])
                out_ref[0, slot, r : r + 8, c : c + 128] = rest_re * scale
                out_ref[1, slot, r : r + 8, c : c + 128] = rest_im * scale
        return carry

    def empty(slot, carry):
        for part in range(2):
            out_ref[part, slot] = jnp.zeros((points, width), F32)
        return carry

    lax.fori_loop(0, count, live, 0)
    lax.fori_loop(count, slots, empty, 0)


def params(mebibytes=24):
    return pltpu.CompilerParams(vmem_limit_bytes=mebibytes * 2**20)


def body(outer, inner, mode_cost, iface_index, basis, radial, axial, flow_coupling, swirl, shift):
    krylov, _, slots, points, width = basis.shape
    modes = mode_cost.shape[0]
    groups = outer * inner
    subs = lax.axis_size("mer")

    def group_of():
        return lax.axis_index("outer") * inner + lax.axis_index("inner")

    def sub_of():
        return lax.axis_index("mer")

    mode = ("outer", "inner")
    shape = jax.ShapeDtypeStruct
    info, to_other, to_pair = pl.pallas_call(
        functools.partial(layout_kernel, group_of, krylov),
        out_shape=(
            shape((2,), jnp.int32),
            shape((2, 2, points, width), F32),
            shape((2, 2, points, width), F32),
        ),
        in_specs=[VMEM, ANY],
        out_specs=(SMEM, VMEM, VMEM),
        scratch_shapes=[pltpu.SemaphoreType.DMA((2, 2))],
        compiler_params=params(52),
        cost_estimate=pl.CostEstimate(flops=10**9, bytes_accessed=2**18, transcendentals=0),
        name="layout",
    )(mode_cost.reshape(-1, math.gcd(modes, 128)), basis)
    other = [(i, i + 1) for i in range(1, groups - 1, 2)]
    other += [(j, i) for i, j in other]
    from_other = lax.ppermute(to_other, mode, other)
    from_pair = lax.ppermute(to_pair, mode, [(i, i ^ 1) for i in range(groups)])

    rows = slots * points
    local, ends, block, radial1, gram, mask = pl.pallas_call(
        functools.partial(inner_kernel, modes),
        out_shape=(
            shape((2, slots, points, width), F32),
            shape((2, 2 * slots, width), F32),
            shape((2, rows, rows), BF16),
            shape((2, width, width), BF16),
            shape((1, 128), F32),
            shape((1, width), F32),
        ),
        in_specs=[SMEM, VMEM, SMEM, VMEM, VMEM, VMEM, VMEM, VMEM],
        out_specs=(VMEM,) * 6,
        scratch_shapes=[pltpu.VMEM((2, rows, width), BF16)] * 2,
        compiler_params=params(),
        cost_estimate=pl.CostEstimate(flops=10**9, bytes_accessed=8 * 2**20, transcendentals=0),
        name="inner",
    )(info, iface_index.reshape(1, -1), shift, basis, radial, axial, flow_coupling, swirl)

    wide = 2 * slots
    local, message = pl.pallas_call(
        functools.partial(halo_kernel, group_of, modes),
        out_shape=(
            shape(local.shape, F32),
            shape((subs, 4 * wide, width), F32),
        ),
        in_specs=[SMEM] + [VMEM] * 9,
        out_specs=(VMEM, VMEM),
        compiler_params=params(),
        name="halo",
    )(info, from_other, from_pair, flow_coupling, block, radial1, ends, axial, mask, local)
    received = lax.all_to_all(message, "mer", 0, 0)

    system = np.diag(np.full(subs - 1, SCHUR_DIAG)) - np.eye(subs - 1, k=1) - np.eye(subs - 1, k=-1)
    w, sums = pl.pallas_call(
        functools.partial(
            project_kernel, sub_of, np.linalg.inv(system), float(width - iface_index.shape[0])
        ),
        out_shape=(shape(local.shape, F32), shape((inner, 1, 128), F32)),
        in_specs=[SMEM] + [VMEM] * 6,
        out_specs=(VMEM, VMEM),
        scratch_shapes=[pltpu.VMEM((4, wide, 8, width), F32)],
        compiler_params=params(),
        name="project",
    )(info, received, mask, axial, basis, gram, local)

    sums = lax.all_to_all(sums, "inner", 0, 0)
    sums = jnp.broadcast_to(jnp.sum(sums, axis=0, keepdims=True), (outer * subs, 1, 128))
    sums = lax.all_to_all(sums, ("outer", "mer"), 0, 0)

    new_vector, coeffs, norm = pl.pallas_call(
        functools.partial(finish_kernel, float(modes * points * subs * width)),
        out_shape=(shape(local.shape, F32), shape((2, krylov), F32), shape((1, 1), F32)),
        in_specs=[SMEM] + [VMEM] * 3,
        compiler_params=params(),
        name="finish",
    )(info, sums, basis, w)
    return new_vector, coeffs, norm.reshape(())


def solution(mesh):
    groups, subs = mesh.devices.shape
    inner = math.gcd(16, groups // 2)
    outer = groups // inner
    fine = Mesh(mesh.devices.reshape(outer, inner, subs), ("outer", "inner", "mer"))
    mode = ("outer", "inner")
    in_specs = (
        P(),
        P(),
        P(None, None, mode, "mer", None),
        P(),
        P(None, "mer", None),
        P(None, "mer", None),
        P("mer", None),
        P(),
    )
    out_specs = (P(None, mode, "mer", None), P(), P())
    return jax.shard_map(
        functools.partial(body, outer, inner),
        mesh=fine,
        in_specs=in_specs,
        out_specs=out_specs,
        check_vma=False,
    )
```
